128 devices in a mesh: dom: 128 (over y, z, x, core).
Axes of the slice: x: 4, y: 4, z: 4, core: 2. Of those that a mesh axis runs over, the one named last changes fastest.
Arguments:
- residual_in: bfloat16 [1024, 32, 1024], P('dom'), may hold values from -6 to 6
- local_inverse: bfloat16 [1024, 1024, 1024], P('dom'), may hold values from -1 to 3, as said below
- coarse_basis: bfloat16 [1024, 16, 1024], P('dom'), may hold values from -0.25 to 0.25
- coarse_inverse: float32 [8192, 8192], P('dom'), may hold values from -1 to 3, as said below
- multiplicity: int32 [1024, 1024], P('dom'), may hold values from 1 to 2, as said below
- iface_len: int32 [1024], P('dom'), may hold values from 1 to 256, as said below
- iface_dof: int32 [1024, 256], P('dom'), may hold values from 0 to 131071, as said below
- coarse_map: int32 [1024, 16], P('dom'), may hold values from 0 to 8191
Outputs:
- first_apply: float32 [1024, 32, 1024], P('dom')
- second_apply: float32 [1024, 32, 1024], P('dom')
The draws below stay inside these ranges and needn't reach their ends.
Inputs may be any that keep to these rules, and one draw needn't show every extreme that they name: `coarse_inverse`: symmetric; diagonal entries dominate. `local_inverse`: diagonal entries dominate. `iface_dof`: subdomain i lies on device i // 8. The live entries of a row are distinct and each is owned (index // 1024) by the row's own device or by the device before it, cyclically; every live index is named by exactly two rows. Dead entries name an index owned by the row's own device. `multiplicity`: 2 on the first iface_len[i] entries of row i, 1 on the others. `iface_len`: the busiest devices carry about twice the mean.
All inputs are finite; a program needn't handle non-finite values.
Results may differ from the reference program's by a relative error of at most 0.00083.
Values sent between devices are 32-bit elements; how exact they have to be, the bound alone decides.
No kernel may reach another device: no remote copies, remote signals or barrier semaphores. Data moves between devices by JAX's collectives and lax.ppermute only.
A program may use at most 128 MiB of HBM per device.

```python
import jax
import jax.numpy as jnp
from jax import lax

L = 1024
LI = 256
CL = 16
R = 32
SUB_DEV = 8
SUBS = 1024
NC = 8192
NI = 131072


def draw_local_inverse(key, part):
    key = jax.random.fold_in(key, 11)
    key_diag, key_off = jax.random.split(key)
    diag = jax.random.uniform(key_diag, (SUBS, L, 1), jnp.float32, 1.0, 2.0)
    off = jnp.clip(jax.random.normal(key_off, (SUBS, L, L), jnp.float32), -4.0, 4.0) * (0.5 / L ** 0.5)
    eye = (jnp.arange(L)[:, None] == jnp.arange(L)[None, :]).astype(jnp.float32)
    return (off * (1.0 - eye) + diag * eye).astype(jnp.bfloat16)


def draw_coarse_inverse(key, part):
    key = jax.random.fold_in(key, 23)
    key_diag, key_off = jax.random.split(key)
    diag = jax.random.uniform(key_diag, (NC, 1), jnp.float32, 1.0, 2.0)
    off = jnp.clip(jax.random.normal(key_off, (NC, NC), jnp.float32), -4.0, 4.0) * (0.35 / NC ** 0.5)
    off = off + off.T
    eye = (jnp.arange(NC)[:, None] == jnp.arange(NC)[None, :]).astype(jnp.float32)
    return off * (1.0 - eye) + diag * eye


def strip_layout(key):
    key = jax.random.fold_in(key, 5)
    key_band, key_around, key_along = jax.random.split(key, 3)
    width = LI // 4
    devices = SUBS // SUB_DEV
    span = max(2, devices // 4)
    subdomain = jnp.arange(SUBS, dtype=jnp.int32)
    device = subdomain // SUB_DEV
    row_index = subdomain % SUB_DEV
    start = jax.random.randint(key_band, (), 0, devices, dtype=jnp.int32)
    thick = (device - start) % devices < span
    around_raw = jax.random.randint(key_around, (SUBS,), width // 4, width // 2 + 1, dtype=jnp.int32)
    along_raw = jax.random.randint(key_along, (SUBS,), width // 4, width // 2 + 1, dtype=jnp.int32)
    around_width = jnp.where(thick, width, around_raw).astype(jnp.int32)
    along_width = (jnp.where(thick, width, along_raw) * (row_index < SUB_DEV - 1)).astype(jnp.int32)
    left_sub = (device - 1) % devices * SUB_DEV + row_index
    lower_sub = jnp.maximum(subdomain - 1, 0)
    left_width = around_width[left_sub]
    lower_width = jnp.where(row_index > 0, along_width[lower_sub], 0).astype(jnp.int32)
    widths = jnp.stack([around_width, along_width, left_width, lower_width], axis=1)
    bases = jnp.stack([subdomain * 2 * width, subdomain * 2 * width + width, left_sub * 2 * width, lower_sub * 2 * width + width], axis=1)
    ends = jnp.cumsum(widths, axis=1).astype(jnp.int32)
    starts = ends - widths
    slot = jnp.arange(LI, dtype=jnp.int32)[None, :]
    which = (slot >= ends[:, 0:1]).astype(jnp.int32) + (slot >= ends[:, 1:2]).astype(jnp.int32) + (slot >= ends[:, 2:3]).astype(jnp.int32)
    index = jnp.take_along_axis(bases - starts, which, axis=1) + slot
    total = ends[:, 3]
    live = slot < total[:, None]
    dof = jnp.where(live, index, (subdomain * 2 * width)[:, None]).astype(jnp.int32)
    return (total, dof)


def draw_iface_len(key, part):
    total, dof = strip_layout(key)
    return total


def draw_iface_dof(key, part):
    total, dof = strip_layout(key)
    return dof


def draw_multiplicity(key, part):
    total, dof = strip_layout(key)
    inside = jnp.arange(L, dtype=jnp.int32)[None, :] < total[:, None]
    return jnp.where(inside, 2, 1).astype(jnp.int32)


def place_ends(drawn, rng, smallest, top_value):
    longest = drawn.shape.index(max(drawn.shape))
    spots = []
    for shift in (0, 1):
        where = [jax.random.randint(jax.random.fold_in(rng, axis), (), 0, length) for axis, length in enumerate(drawn.shape)]
        where[longest] = (where[longest] + shift) % drawn.shape[longest]
        spots.append(tuple(where))
    return drawn.at[spots[0]].set(smallest).at[spots[1]].set(top_value)


def steps_of(key, shape, cuts, smallest, top_value):
    factor_of, own = 1.0, jax.random.fold_in(key, 6)
    for axis_at, parts in cuts:
        draws = jnp.exp(jax.random.uniform(jax.random.fold_in(own, axis_at), (parts,), jnp.float32, smallest / len(cuts), top_value / len(cuts)))
        factor_of = factor_of * jnp.repeat(draws, shape[axis_at] // parts).reshape([-1 if axis == axis_at else 1 for axis in range(len(shape))])
    return factor_of


def noise(stream_key, dims, scale, bound, shards=(), kind=jnp.bfloat16):
    level = steps_of(stream_key, dims, shards, -0.22, 0.18) if shards else 1.0
    array = jax.random.normal(stream_key, dims, jnp.float32) * scale * level
    return jnp.minimum(jnp.maximum(array, -bound), bound).astype(kind)


def setup_inputs(seed: int = 0) -> dict:
    keys = jax.random.split(jax.random.key(seed), 9)
    residual_in = noise(keys[0], (SUBS, R, L), 1.0, 6.0, ((0, 128),))
    local_inverse = draw_local_inverse(jax.random.fold_in(keys[8], 71), 0)
    coarse_basis = noise(keys[2], (SUBS, CL, L), (L // 2) ** -0.5, 0.25, ((0, 128),))
    coarse_inverse = draw_coarse_inverse(jax.random.fold_in(keys[8], 71), 0)
    multiplicity = draw_multiplicity(jax.random.fold_in(keys[8], 71), 0)
    iface_len = draw_iface_len(jax.random.fold_in(keys[8], 71), 0)
    iface_dof = draw_iface_dof(jax.random.fold_in(keys[8], 71), 0)
    coarse_map = place_ends(jax.random.randint(keys[7], (SUBS, CL), 0, NC), jax.random.fold_in(keys[7], 1), 0, NC - 1).astype(jnp.int32)
    return {"residual_in": residual_in, "local_inverse": local_inverse, "coarse_basis": coarse_basis, "coarse_inverse": coarse_inverse, "multiplicity": multiplicity, "iface_len": iface_len, "iface_dof": iface_dof, "coarse_map": coarse_map}


def precondition(values, local_inverse, coarse_basis, coarse_inverse, weights, live, iface_dof, coarse_map):
    scaled = (values * weights[:, None, :]).astype(jnp.bfloat16)
    basis32 = coarse_basis.astype(jnp.float32)
    coarse_part = jnp.einsum("srl,skl->srk", scaled.astype(jnp.float32), basis32, precision=lax.Precision.HIGHEST)
    flat_part = jnp.transpose(coarse_part, (1, 0, 2)).reshape(R, -1)
    coarse_rhs = jnp.zeros((R, NC), jnp.float32).at[:, coarse_map.reshape(-1)].add(flat_part)
    coarse_sol = jnp.dot(coarse_rhs, coarse_inverse.T, precision=lax.Precision.HIGHEST)
    looked = coarse_sol[:, coarse_map]
    correction = jnp.einsum("rsk,skl->srl", looked, basis32, precision=lax.Precision.HIGHEST)

    def local_solve(pair):
        return jnp.dot(pair[0], pair[1], preferred_element_type=jnp.float32)

    combined = lax.map(local_solve, (scaled, local_inverse)) + correction
    contrib = combined[:, :, :LI] * weights[:, None, :LI] * live[:, None, :]
    flat_contrib = jnp.transpose(contrib, (1, 0, 2)).reshape(R, -1)
    assembled = jnp.zeros((R, NI), jnp.float32).at[:, iface_dof.reshape(-1)].add(flat_contrib)
    fetched = jnp.transpose(assembled[:, iface_dof], (1, 0, 2))
    head = jnp.where(live[:, None, :] > 0, fetched, combined[:, :, :LI])
    return jnp.concatenate([head, combined[:, :, LI:]], axis=2)


def reference(residual_in, local_inverse, coarse_basis, coarse_inverse, multiplicity, iface_len, iface_dof, coarse_map):
    weights = 1.0 / multiplicity.astype(jnp.float32)
    live = (jnp.arange(LI, dtype=jnp.int32)[None, :] < iface_len[:, None]).astype(jnp.float32)
    first_apply = precondition(residual_in.astype(jnp.float32), local_inverse, coarse_basis, coarse_inverse, weights, live, iface_dof, coarse_map)
    second_apply = precondition(first_apply, local_inverse, coarse_basis, coarse_inverse, weights, live, iface_dof, coarse_map)
    return first_apply, second_apply
```

```python
import functools

import jax
import jax.numpy as jnp
from jax import lax
from jax.experimental import pallas as pl
from jax.experimental.pallas import tpu as pltpu
from jax.sharding import Mesh
from jax.sharding import PartitionSpec as P

CHIPS = ("y", "z", "x")
DOM = ("y", "z", "x", "c")
MIB = 2**20
VMEM = pl.BlockSpec(memory_space=pltpu.VMEM)
SMEM = pl.BlockSpec(memory_space=pltpu.SMEM)


def halves(value):
    high = value.astype(jnp.bfloat16)
    low = (value - high.astype(jnp.float32)).astype(jnp.bfloat16)
    return jnp.concatenate([high, low], axis=0)


def thirds(value):
    high = value.astype(jnp.bfloat16)
    rest = value - high.astype(jnp.float32)
    middle = rest.astype(jnp.bfloat16)
    low = (rest - middle.astype(jnp.float32)).astype(jnp.bfloat16)
    return jnp.concatenate([high, middle, low], axis=0)


def split_dot(value, parts, other, contract=0):
    rows = value.shape[0]
    pieces = halves(value) if parts == 2 else thirds(value)
    out = lax.dot_general(
        pieces, other, (((1,), (contract,)), ((), ())), preferred_element_type=jnp.float32
    )
    total = out[:rows]
    for part in range(1, parts):
        total = total + out[part * rows : (part + 1) * rows]
    return total


def call(kernel, out_shape, args, specs=None, mib=40, **more):
    return pl.pallas_call(
        kernel,
        out_shape=out_shape,
        in_specs=specs if specs is not None else [VMEM] * len(args),
        compiler_params=pltpu.CompilerParams(vmem_limit_bytes=mib * MIB),
        **more,
    )(*args)


def f32(*shape):
    return jax.ShapeDtypeStruct(shape, jnp.float32)


def bf16(*shape):
    return jax.ShapeDtypeStruct(shape, jnp.bfloat16)


def turn_kernel(core_ref, mine_ref, other_ref, out_ref):
    core = core_ref[0]
    for chunk in range(mine_ref.shape[1] // 128):
        columns = slice(chunk * 128, (chunk + 1) * 128)
        mine, other = mine_ref[:, columns], other_ref[:, columns]
        first = jnp.where(core == 0, mine, other)
        second = jnp.where(core == 0, other, mine)
        out_ref[columns, :] = jnp.concatenate([first, second], axis=0).T


def pick_kernel(index_ref, turned_ref, out_ref, rows_ref):
    count = rows_ref.shape[0]
    start = pl.program_id(0) * count

    def sixteen(group, carry):
        for row in range(16):
            place = group * 16 + row
            rows_ref[pl.ds(place, 1), :] = turned_ref[pl.ds(index_ref[start + place], 1), :]
        return carry

    lax.fori_loop(0, count // 16, sixteen, 0)
    rows = rows_ref[...]
    high = rows.astype(jnp.bfloat16)
    width = rows.shape[1]
    out_ref[:, :width] = high
    out_ref[:, width:] = (rows - high.astype(jnp.float32)).astype(jnp.bfloat16)


def pick(index, turned):
    count, block = index.shape[0], 1024
    order, width = turned.shape
    return pl.pallas_call(
        pick_kernel,
        out_shape=bf16(count, 2 * width),
        grid_spec=pltpu.PrefetchScalarGridSpec(
            num_scalar_prefetch=1,
            grid=(count // block,),
            in_specs=[
                pl.BlockSpec((order, width), lambda i, s: (0, 0), pipeline_mode=pl.Buffered(1))
            ],
            out_specs=pl.BlockSpec((block, 2 * width), lambda i, s: (i, 0)),
            scratch_shapes=[pltpu.VMEM((block, width), jnp.float32)],
        ),
        compiler_params=pltpu.CompilerParams(vmem_limit_bytes=24 * MIB),
        cost_estimate=pl.CostEstimate(flops=0, bytes_accessed=60 * MIB, transcendentals=0),
        name="pick",
    )(index, turned)


def solve_kernel(parts_ref, picked_ref, out_ref):
    cases = parts_ref.shape[1]
    width = out_ref.shape[2]
    total = jnp.zeros((2 * cases, 2 * width), jnp.float32)
    for pair in range(parts_ref.shape[0] // 2):
        value = jnp.concatenate([parts_ref[2 * pair], parts_ref[2 * pair + 1]], axis=1)
        wide = value.shape[1]
        total = total + jnp.dot(
            halves(value),
            picked_ref[pair * wide : (pair + 1) * wide, :],
            preferred_element_type=jnp.float32,
        )
    high, low = total[:cases], total[cases:]
    own = (high[:, :width] + high[:, width:]) + (low[:, :width] + low[:, width:])
    out_ref[...] = jnp.broadcast_to(own[None], out_ref.shape)


def local_kernel(scaled_ref, inverse_ref, slots_ref, mask_ref, local_ref, sums_ref):
    solved = jnp.dot(scaled_ref[0], inverse_ref[0], preferred_element_type=jnp.float32)
    local_ref[0] = solved
    width = slots_ref.shape[0]
    sums = split_dot(solved[:, :width] * mask_ref[0], 3, slots_ref[...])

    @pl.when(pl.program_id(0) == 0)
    def _():
        sums_ref[...] = sums

    @pl.when(pl.program_id(0) > 0)
    def _():
        sums_ref[...] += sums


def local_solve(scaled, inverse, slots, mask):
    subs, cases, length = scaled.shape
    width = slots.shape[0] // subs
    return pl.pallas_call(
        local_kernel,
        out_shape=(f32(subs, cases, length), f32(cases, slots.shape[1])),
        grid=(subs,),
        in_specs=[
            pl.BlockSpec((1, cases, length), lambda i: (i, 0, 0)),
            pl.BlockSpec((1, length, length), lambda i: (i, 0, 0)),
            pl.BlockSpec((width, slots.shape[1]), lambda i: (i, 0)),
            pl.BlockSpec((1, 1, width), lambda i: (i, 0, 0)),
        ],
        out_specs=(
            pl.BlockSpec((1, cases, length), lambda i: (i, 0, 0)),
            pl.BlockSpec((cases, slots.shape[1]), lambda i: (0, 0)),
        ),
        compiler_params=pltpu.CompilerParams(vmem_limit_bytes=24 * MIB),
        cost_estimate=pl.CostEstimate(
            flops=2 * subs * cases * length * length,
            bytes_accessed=36 * MIB,
            transcendentals=0,
        ),
        name="local_solve",
    )(scaled, inverse, slots, mask)


def base_kernel(local_ref, sums_ref, prev_ref, next_ref, slots_ref, live_ref, base_ref):
    half = prev_ref.shape[1]
    sums = sums_ref[...]
    sums = jnp.concatenate(
        [sums[:, :half] + next_ref[...], sums[:, half:] + prev_ref[...]], axis=1
    )
    width = live_ref.shape[2]
    for sub in range(local_ref.shape[0]):
        fetched = split_dot(sums, 3, slots_ref[sub * width : (sub + 1) * width, :], 1)
        base_ref[sub, :, :width] = jnp.where(
            live_ref[sub] > 0, fetched, local_ref[sub, :, :width]
        )
        base_ref[sub, :, width:] = local_ref[sub, :, width:]


def make_base(local, sums, behind, ahead, slots, live):
    return call(
        base_kernel,
        f32(*local.shape),
        (local, sums, behind, ahead, slots, live),
        cost_estimate=pl.CostEstimate(
            flops=2 * 3 * 32 * 2048 * 2048, bytes_accessed=14 * MIB, transcendentals=0
        ),
        name="make_base",
    )


def own_parts(scaled_of, basis_ref):
    total = None
    for sub in range(basis_ref.shape[0]):
        part = lax.dot_general(
            scaled_of(sub),
            basis_ref[sub],
            (((1,), (1,)), ((), ())),
            preferred_element_type=jnp.float32,
        )
        total = part if total is None else total + part
    return total


def spread(parts, out_ref):
    cases = out_ref.shape[1]
    for core in range(2):
        own = parts[core * cases : (core + 1) * cases]
        for chip in range(out_ref.shape[0] // 2):
            out_ref[2 * chip + core] = own


def first_kernel(values_ref, weights_ref, basis_ref, scaled_ref, parts_ref):
    for sub in range(values_ref.shape[0]):
        scaled = values_ref[sub].astype(jnp.float32) * weights_ref[sub]
        scaled_ref[sub] = scaled.astype(jnp.bfloat16)
    spread(own_parts(lambda sub: scaled_ref[sub], basis_ref), parts_ref)


def correct(core_ref, mine_ref, other_ref, hot_ref, shared_ref, basis_ref, base_ref, out_ref):
    subs, cases, _ = base_ref.shape
    width = shared_ref.shape[1] // subs
    chips, half, rows = mine_ref.shape
    looked = jnp.zeros((4 * half, hot_ref.shape[1]), jnp.float32)
    for pair in range(chips // 2):
        mine = jnp.concatenate([mine_ref[2 * pair], mine_ref[2 * pair + 1]], axis=1)
        other = jnp.concatenate([other_ref[2 * pair], other_ref[2 * pair + 1]], axis=1)
        both = jnp.concatenate([mine, other], axis=0)
        looked = looked + jnp.dot(
            halves(both),
            hot_ref[2 * pair * rows : 2 * (pair + 1) * rows, :],
            preferred_element_type=jnp.float32,
        )
    looked = looked[: 2 * half] + looked[2 * half :]
    turned = jnp.concatenate([looked[half:], looked[:half]], axis=0)
    looked = jnp.where(core_ref[0] == 0, looked, turned)
    own = looked.shape[1] // 3
    shared = split_dot(looked, 3, shared_ref[...])
    for sub in range(subs):
        inner = split_dot(looked[:, own : 2 * own], 3, basis_ref[sub, :, width:])
        out_ref[sub, :, :width] = (
            base_ref[sub, :, :width] + shared[:, sub * width : (sub + 1) * width]
        )
        out_ref[sub, :, width:] = base_ref[sub, :, width:] + inner


def last_kernel(core_ref, mine_ref, other_ref, hot_ref, shared_ref, basis_ref, base_ref, out_ref):
    correct(core_ref, mine_ref, other_ref, hot_ref, shared_ref, basis_ref, base_ref, out_ref)


def middle_kernel(
    core_ref,
    mine_ref,
    other_ref,
    hot_ref,
    shared_ref,
    basis_ref,
    base_ref,
    weights_ref,
    out_ref,
    scaled_ref,
    parts_ref,
):
    correct(core_ref, mine_ref, other_ref, hot_ref, shared_ref, basis_ref, base_ref, out_ref)
    for sub in range(base_ref.shape[0]):
        scaled_ref[sub] = (out_ref[sub] * weights_ref[sub]).astype(jnp.bfloat16)
    spread(own_parts(lambda sub: scaled_ref[sub], basis_ref), parts_ref)


def shift(value, steps):
    count = lax.axis_size(DOM)
    return lax.ppermute(value, DOM, [(s, (s + steps) % count) for s in range(count)])


def swap(value):
    return lax.ppermute(value, "c", [(0, 1), (1, 0)])


def local(
    residual_in,
    local_inverse,
    coarse_basis,
    coarse_inverse,
    multiplicity,
    iface_len,
    iface_dof,
    coarse_map,
):
    subs, cases, length = residual_in.shape
    coarse = coarse_basis.shape[1]
    width = iface_dof.shape[1]
    order = coarse_inverse.shape[1]
    count = lax.axis_size(DOM)
    chips = count // 2
    half_cases = cases // 2
    entries = subs * coarse
    spots = subs * width
    owned = spots // 2
    device = lax.axis_index(DOM)
    core = lax.axis_index("c").astype(jnp.int32).reshape(1)

    own_map = coarse_map.reshape(1, entries)
    maps = lax.all_to_all(jnp.broadcast_to(own_map, (count, entries)), DOM, 0, 0, tiled=True)
    turned = call(
        turn_kernel,
        f32(order, 2 * coarse_inverse.shape[0]),
        (core, coarse_inverse, swap(coarse_inverse)),
        [SMEM, VMEM, VMEM],
        mib=24,
        name="turn",
    )

    weights = 1.0 / multiplicity.astype(jnp.float32)
    weights3 = weights.reshape(subs, 1, length)
    same = (
        jnp.arange(subs, dtype=jnp.int32)[:, None] == jnp.arange(subs, dtype=jnp.int32)[None, :]
    )
    basis_pad = jnp.where(
        same[:, :, None, None], coarse_basis[:, None], jnp.zeros((), jnp.bfloat16)
    ).reshape(subs, entries, length)

    scaled, parts = call(
        first_kernel,
        (bf16(subs, cases, length), f32(count, half_cases, entries)),
        (residual_in, weights3, basis_pad),
        mib=24,
        name="first",
    )
    parts = lax.all_to_all(parts, DOM, 0, 0, tiled=True)

    live = jnp.arange(width, dtype=jnp.int32)[None, :] < iface_len[:, None]
    owner = iface_dof // owned
    slot = jnp.where(owner != device, owned, 0) + (iface_dof - owner * owned)
    slot = jnp.where(live, slot, -1).reshape(spots)
    slots = (slot[:, None] == jnp.arange(spots, dtype=jnp.int32)[None, :]).astype(jnp.bfloat16)
    live3 = live.astype(jnp.float32).reshape(subs, 1, width)
    mask = live3 * weights3[:, :, :width]

    def interface(scaled):
        solved, sums = local_solve(scaled, local_inverse, slots, mask)
        ahead = shift(sums[:, owned:], -1)
        behind = shift(sums[:, :owned], 1)
        return make_base(solved, sums, behind, ahead, slots, live3)

    base = interface(scaled)

    head = coarse_basis[:, :, :width].astype(jnp.float32)
    weighted = (head * mask).astype(jnp.bfloat16)
    compact = jnp.transpose(weighted, (1, 0, 2)).reshape(coarse, spots)
    row_of = jnp.broadcast_to(jnp.arange(subs, dtype=jnp.bfloat16)[:, None], (subs, width))
    block = jnp.where(
        same[:, None, :, None], weighted[:, :, None, :], jnp.zeros((), jnp.bfloat16)
    ).reshape(entries, spots)
    stacked = jnp.concatenate(
        [block, compact, row_of.reshape(1, spots), jnp.zeros((15, spots), jnp.bfloat16)], axis=0
    )
    by_slot = jnp.dot(stacked, slots, preferred_element_type=jnp.float32)
    compact = by_slot[entries : entries + 24]
    ahead = shift(compact[:, owned:], -1)
    behind = shift(compact[:, :owned], 1)

    def widened(arrived):
        row = arrived[coarse : coarse + 1]
        subs_of = jnp.arange(subs, dtype=jnp.float32)[:, None, None]
        return jnp.where(row[None] == subs_of, arrived[None, :coarse], 0.0).reshape(
            entries, owned
        )

    nothing = jnp.zeros((entries, owned), jnp.float32)
    by_slot = jnp.concatenate(
        [
            jnp.concatenate([nothing, widened(behind)], axis=1),
            by_slot[:entries],
            jnp.concatenate([widened(ahead), nothing], axis=1),
        ],
        axis=0,
    ).astype(jnp.bfloat16)
    shared = lax.dot_general(
        by_slot, slots, (((1,), (1,)), ((), ())), preferred_element_type=jnp.float32
    )
    dead = jnp.where(
        same[:, None, :, None] & ~live[None, None], head[:, :, None, :], 0.0
    ).reshape(entries, spots)
    shared = (
        (shared + jnp.concatenate([jnp.zeros_like(dead), dead, jnp.zeros_like(dead)], axis=0))
    ).astype(jnp.bfloat16)

    near = [
        lax.dynamic_slice_in_dim(maps, (device + step) % count, 1, axis=0)
        for step in (count - 1, 0, 1)
    ]
    near = jnp.concatenate(near, axis=1)
    hot = (jnp.arange(order, dtype=jnp.int32)[:, None] == near).astype(jnp.bfloat16)
    picked = pick(maps.reshape(count * entries), turned)

    def coarse_solve(parts):
        own = call(
            solve_kernel,
            f32(chips, half_cases, 2 * coarse_inverse.shape[0]),
            (parts, picked),
            name="solve",
        )
        mine = lax.all_to_all(own, CHIPS, 0, 0, tiled=True)
        return mine, swap(mine)

    specs = [SMEM] + [VMEM] * 6
    mine, other = coarse_solve(parts)
    first_apply, scaled, parts = call(
        middle_kernel,
        (
            f32(subs, cases, length),
            bf16(subs, cases, length),
            f32(count, half_cases, entries),
        ),
        (core, mine, other, hot, shared, basis_pad, base, weights3),
        specs + [VMEM],
        name="middle",
    )
    parts = lax.all_to_all(parts, DOM, 0, 0, tiled=True)
    base = interface(scaled)
    mine, other = coarse_solve(parts)
    second_apply = call(
        last_kernel,
        f32(subs, cases, length),
        (core, mine, other, hot, shared, basis_pad, base),
        specs,
        name="last",
    )
    return first_apply, second_apply


def solution(mesh):
    grid = Mesh(mesh.devices.reshape(4, 4, 4, 2), DOM)
    placed = (
        P(DOM, None, None),
        P(DOM, None, None),
        P(DOM, None, None),
        P(DOM, None),
        P(DOM, None),
        P(DOM),
        P(DOM, None),
        P(DOM, None),
    )
    return jax.shard_map(
        local,
        mesh=grid,
        in_specs=placed,
        out_specs=(P(DOM, None, None), P(DOM, None, None)),
        check_vma=False,
    )
```

```python
import jax
import jax.numpy as jnp
from jax import lax
from jax.experimental import pallas as pl
from jax.experimental.pallas import tpu as pltpu
from jax.sharding import Mesh
from jax.sharding import PartitionSpec as P

CHIPS = ("y", "z", "x")
DOM = ("y", "z", "x", "c")
MIB = 2**20
VMEM = pl.BlockSpec(memory_space=pltpu.VMEM)
SMEM = pl.BlockSpec(memory_space=pltpu.SMEM)
ANY = pl.BlockSpec(memory_space=pl.ANY)
HBM = pl.BlockSpec(memory_space=pltpu.HBM)
BY_ROW = (((1,), (1,)), ((), ()))


def halves(value):
    high = value.astype(jnp.bfloat16)
    low = (value - high.astype(jnp.float32)).astype(jnp.bfloat16)
    return jnp.concatenate([high, low], axis=0)


def thirds(value):
    high = value.astype(jnp.bfloat16)
    rest = value - high.astype(jnp.float32)
    middle = rest.astype(jnp.bfloat16)
    low = (rest - middle.astype(jnp.float32)).astype(jnp.bfloat16)
    return jnp.concatenate([high, middle, low], axis=0)


def folded(out, rows):
    total = out[:rows]
    for start in range(rows, out.shape[0], rows):
        total = total + out[start : start + rows]
    return total


def mul(left, right):
    return jnp.dot(left, right, preferred_element_type=jnp.float32)


def mul_rows(left, right):
    return lax.dot_general(left, right, BY_ROW, preferred_element_type=jnp.float32)


def call(kernel, name, out_shape, args, specs, flops=1e6, moved=MIB, mib=16, **more):
    return pl.pallas_call(
        kernel,
        out_shape=out_shape,
        in_specs=specs,
        compiler_params=pltpu.CompilerParams(vmem_limit_bytes=mib * MIB),
        cost_estimate=pl.CostEstimate(
            flops=int(flops), bytes_accessed=int(moved), transcendentals=0
        ),
        name=name,
        **more,
    )(*args)


def f32(*shape):
    return jax.ShapeDtypeStruct(shape, jnp.float32)


def bf16(*shape):
    return jax.ShapeDtypeStruct(shape, jnp.bfloat16)


def weights_of(multiplicity):
    return 1.0 / multiplicity.astype(jnp.float32)


def part_out(core_ref, scaled_ref, basis_ref, keep_ref, send_ref):
    parts = mul_rows(scaled_ref[0], basis_ref[0])
    for sub in range(1, basis_ref.shape[0]):
        parts = parts + mul_rows(scaled_ref[sub], basis_ref[sub])
    half = keep_ref.shape[0]
    first = core_ref[0] == 0
    keep_ref[...] = jnp.where(first, parts[:half], parts[half:])
    send_ref[...] = jnp.where(first, parts[half:], parts[:half])


def widen(basis_ref, wide_ref):
    subs, coarse, _ = basis_ref.shape
    for sub in range(subs):
        wide_ref[sub] = jnp.zeros_like(wide_ref[sub])
        wide_ref[sub, sub * coarse : (sub + 1) * coarse] = basis_ref[sub]


def first_kernel(
    core_ref, values_ref, mult_ref, basis_ref, scaled_ref, keep_ref, send_ref, wide_ref
):
    widen(basis_ref, wide_ref)
    for sub in range(values_ref.shape[0]):
        scaled = values_ref[sub].astype(jnp.float32) * weights_of(mult_ref[sub : sub + 1])
        scaled_ref[sub] = scaled.astype(jnp.bfloat16)
    part_out(core_ref, scaled_ref, wide_ref, keep_ref, send_ref)


def hot_pair(maps, pair):
    rows = lax.broadcasted_iota(jnp.int32, (256, maps.shape[1]), 0) + 256 * pair
    return jnp.where(rows == maps, 1.0, 0.0).astype(jnp.bfloat16)


def columns_of(rows):
    if rows.shape[0] == 1:
        rows = jnp.broadcast_to(rows, (8, rows.shape[1]))
    return rows.astype(jnp.float32).T


def dense_kernel(own_ref, mate_ref, keep_ref, got_ref, *refs):
    out_ref = refs[-1]
    cases, width = keep_ref.shape
    value = halves(jnp.concatenate([keep_ref[...], got_ref[...]], axis=1))
    maps = jnp.concatenate([own_ref[...], mate_ref[...]], axis=1)
    maps = columns_of(maps)[:, :1]
    wide = 2 * out_ref.shape[2]
    for pair in range(out_ref.shape[0] // 2):
        numbers = lax.broadcasted_iota(jnp.int32, (maps.shape[0], wide), 1) + wide * pair
        hot = jnp.where(numbers.astype(jnp.float32) == maps, 1.0, 0.0).astype(jnp.bfloat16)
        part = folded(mul(value, hot), cases)
        out_ref[2 * pair] = part[:, : wide // 2]
        out_ref[2 * pair + 1] = part[:, wide // 2 :]


def sum_kernel(parts_ref, *refs):
    out_ref = refs[-1]
    total = parts_ref[0]
    for chip in range(1, parts_ref.shape[0]):
        total = total + parts_ref[chip]
    for chip in range(out_ref.shape[0]):
        out_ref[chip] = total


def solve_kernel(core_ref, rhs_ref, mine_ref, other_ref, out_ref):
    cases, width = rhs_ref.shape[1:]
    total = jnp.zeros((2 * cases, 4 * mine_ref.shape[0]), jnp.float32)
    for pair in range(rhs_ref.shape[0] // 2):
        value = jnp.concatenate([rhs_ref[2 * pair], rhs_ref[2 * pair + 1]], axis=1)
        columns = slice(2 * pair * width, 2 * (pair + 1) * width)
        rows = jnp.concatenate([mine_ref[:, columns], other_ref[:, columns]], axis=0)
        total = total + mul_rows(halves(value), halves(rows))
    total = folded(total, cases)
    own = total[:, :width] + total[:, width:]
    half = width // 2
    turned = jnp.concatenate([own[:, half:], own[:, :half]], axis=1)
    own = jnp.where(core_ref[0] == 0, own, turned)
    for chip in range(out_ref.shape[0]):
        out_ref[chip] = own


def live_of(len_ref, sub, width):
    return lax.broadcasted_iota(jnp.int32, (1, width), 1) < len_ref[sub]


def slot_row(place_ref, len_ref, dof_ref, sub, spots):
    owned = spots // 2
    dof = dof_ref[sub : sub + 1]
    owner = lax.div(dof, owned)
    away = (owner != place_ref[0]).astype(jnp.int32)
    far = jnp.where(place_ref[1] == 0, away, 1 - away)
    live = live_of(len_ref, sub, dof.shape[1])
    return jnp.where(live, far * owned + (dof - owner * owned), -1)


def slots_of(place_ref, len_ref, dof_ref, sub, spots):
    slot = slot_row(place_ref, len_ref, dof_ref, sub, spots)
    rows = lax.broadcasted_iota(jnp.int32, (spots, slot.shape[1]), 0)
    return jnp.where(rows == slot, 1.0, 0.0).astype(jnp.bfloat16)


def column_copies(inverse_ref, buffer_ref, sems, start):
    copies = []
    for sub in range(inverse_ref.shape[0]):
        columns = pl.ds(start, buffer_ref.shape[2])
        copies.append(
            pltpu.make_async_copy(
                inverse_ref.at[sub, :, columns], buffer_ref.at[sub], sems.at[sub]
            )
        )
    for copy in copies:
        copy.start()
    return copies


def edge_kernel(place_ref, len_ref, scaled_ref, mult_ref, dof_ref, inverse_ref, *refs):
    *inputs, edge_ref, mate_ref, far_ref, buffer_ref, sems = refs
    subs, cases, _ = scaled_ref.shape
    width = dof_ref.shape[1]
    owned = mate_ref.shape[1]
    copies = column_copies(inverse_ref, buffer_ref, sems, 0)
    mate_ref[...] = jnp.zeros_like(mate_ref)
    far_ref[...] = jnp.zeros_like(far_ref)
    if inputs:
        basis_ref, map_ref, own_ref = inputs
        coarse = basis_ref.shape[1]
        for ref in (mate_ref, far_ref):
            ref[cases + coarse + 8 : cases + coarse + 9, : map_ref.shape[1]] = map_ref[
                ...
            ].astype(jnp.float32)
    slots = [slot_row(place_ref, len_ref, dof_ref, sub, 2 * owned) for sub in range(subs)]
    slots = columns_of(jnp.concatenate(slots, axis=0))
    numbers = lax.broadcasted_iota(jnp.int32, (width, 2 * owned), 1).astype(jnp.float32)
    for sub in range(subs):
        hot = jnp.where(numbers == slots[:, sub : sub + 1], 1.0, 0.0).astype(jnp.bfloat16)
        live = live_of(len_ref, sub, width)
        mask = jnp.where(live, weights_of(mult_ref[sub : sub + 1, :width]), 0.0)
        copies[sub].wait()
        solved = mul(scaled_ref[sub], buffer_ref[sub])
        edge_ref[:, sub * width : (sub + 1) * width] = solved
        pieces = [thirds(solved * mask)]
        if inputs:
            pieces.append((basis_ref[sub, :, :width].astype(jnp.float32) * mask).astype(jnp.bfloat16))
            number = jnp.where(live, float(sub), 0.0).astype(jnp.bfloat16)
            pieces.append(jnp.broadcast_to(number, (16, width)))
        out = mul(jnp.concatenate(pieces, axis=0), hot)
        moved = folded(out[: 3 * cases], cases)
        if inputs:
            rest = out[3 * cases : 3 * cases + coarse + 8]
            own_ref[sub * coarse : (sub + 1) * coarse, :] = rest[:coarse].astype(jnp.bfloat16)
            moved = jnp.concatenate([moved, rest], axis=0)
        mate_ref[: moved.shape[0]] += moved[:, :owned]
        far_ref[: moved.shape[0]] += moved[:, owned:]


def inner_kernel(scaled_ref, inverse_ref, after_ref, after_too_ref, inner_ref, buffer_ref, sems):
    copies = column_copies(
        inverse_ref, buffer_ref, sems, inverse_ref.shape[2] - buffer_ref.shape[2]
    )
    for sub in range(scaled_ref.shape[0]):
        copies[sub].wait()
        inner_ref[sub] = mul(scaled_ref[sub], buffer_ref[sub])


def head_kernel(
    place_ref,
    len_ref,
    edge_ref,
    mate_ref,
    far_ref,
    from_mate_ref,
    from_far_ref,
    dof_ref,
    after_ref,
    head_ref,
):
    subs, width = dof_ref.shape
    cases = edge_ref.shape[0]
    sums = thirds(
        jnp.concatenate(
            [
                mate_ref[:cases] + from_mate_ref[:cases],
                far_ref[:cases] + from_far_ref[:cases],
            ],
            axis=1,
        )
    )
    for sub in range(subs):
        columns = slice(sub * width, (sub + 1) * width)
        hot = slots_of(place_ref, len_ref, dof_ref, sub, sums.shape[1])
        fetched = folded(mul(sums, hot), cases)
        head_ref[:, columns] = jnp.where(
            live_of(len_ref, sub, width), fetched, edge_ref[:, columns]
        )


def share_kernel(
    place_ref,
    len_ref,
    own_ref,
    from_mate_ref,
    from_far_ref,
    dof_ref,
    basis_ref,
    after_ref,
    shared_ref,
    map_ref,
    first_ref,
    second_ref,
):
    subs, coarse, _ = basis_ref.shape
    entries, spots = own_ref.shape
    owned = spots // 2
    width = dof_ref.shape[1]
    cases = from_mate_ref.shape[0] - 16 - coarse
    for ref, arrived, start in ((first_ref, from_mate_ref, 0), (second_ref, from_far_ref, owned)):
        ref[:entries] = own_ref[:, start : start + owned]
        row = arrived[cases + coarse : cases + coarse + 1]
        basis = arrived[cases : cases + coarse]
        for sub in range(subs):
            ref[entries + sub * coarse : entries + (sub + 1) * coarse] = jnp.where(
                row == sub, basis, 0.0
            ).astype(jnp.bfloat16)
    for sub in range(subs):
        columns = slice(sub * width, (sub + 1) * width)
        hot = slots_of(place_ref, len_ref, dof_ref, sub, spots)
        mate = mul(first_ref[...], hot[:owned])
        far = mul(second_ref[...], hot[owned:])
        own = mate[:entries] + far[:entries]
        rows = slice(sub * coarse, (sub + 1) * coarse)
        full = jnp.concatenate([own, mate[entries:], far[entries:]], axis=0)
        shared_ref[:, columns] = full.astype(jnp.bfloat16)
        dead = jnp.where(
            live_of(len_ref, sub, width), 0.0, basis_ref[sub, :, :width].astype(jnp.float32)
        )
        shared_ref[rows, columns] = (own[rows] + dead).astype(jnp.bfloat16)
    number = from_far_ref[cases + coarse + 8 : cases + coarse + 9, :entries]
    map_ref[...] = number.astype(jnp.int32)


def correct_kernel(
    core_ref,
    own_ref,
    mate_ref,
    far_ref,
    mine_ref,
    other_ref,
    basis_ref,
    head_ref,
    shared_hbm,
    inner_hbm,
    *refs,
):
    *inputs, wide_ref, shared_ref, inner_ref, values_ref, sems = refs
    out_hbm = inputs[0] if len(inputs) == 1 else inputs[1]
    subs, cases, _ = values_ref.shape
    chips, half, _ = mine_ref.shape
    entries = own_ref.shape[1]
    width = head_ref.shape[1] // subs
    arrive = [
        pltpu.make_async_copy(shared_hbm, shared_ref, sems.at[0]),
        pltpu.make_async_copy(inner_hbm, inner_ref, sems.at[1]),
    ]
    leave = [
        pltpu.make_async_copy(values_ref.at[sub], out_hbm.at[sub], sems.at[2 + sub])
        for sub in range(subs)
    ]
    for copy in arrive:
        copy.start()
    widen(basis_ref, wide_ref)
    maps = jnp.concatenate([own_ref[...], mate_ref[...], far_ref[...]], axis=1)
    looked = jnp.zeros((4 * half, 3 * entries), jnp.float32)
    for pair in range(chips // 2):
        mine = jnp.concatenate([mine_ref[2 * pair], mine_ref[2 * pair + 1]], axis=1)
        other = jnp.concatenate([other_ref[2 * pair], other_ref[2 * pair + 1]], axis=1)
        both = halves(jnp.concatenate([mine, other], axis=0))
        looked = looked + mul(both, hot_pair(maps, pair))
    looked = folded(looked, cases)
    turned = jnp.concatenate([looked[half:], looked[:half]], axis=0)
    looked = jnp.where(core_ref[0] == 0, looked, turned)
    own = thirds(looked[:, :entries])
    looked = thirds(looked)
    for copy in arrive:
        copy.wait()
    for sub in range(subs):
        columns = slice(sub * width, (sub + 1) * width)
        values_ref[sub, :, :width] = head_ref[:, columns] + folded(
            mul(looked, shared_ref[:, columns]), cases
        )
        values_ref[sub, :, width:] = inner_ref[sub] + folded(
            mul(own, wide_ref[sub, :, width:]), cases
        )
        leave[sub].start()
    if len(inputs) > 1:
        mult_ref, _, scaled_ref, keep_ref, send_ref = inputs
        for sub in range(subs):
            scaled = values_ref[sub] * weights_of(mult_ref[sub : sub + 1])
            scaled_ref[sub] = scaled.astype(jnp.bfloat16)
        part_out(core_ref, scaled_ref, wide_ref, keep_ref, send_ref)
    for copy in leave:
        copy.wait()


def swap(value):
    return lax.ppermute(value, "c", [(0, 1), (1, 0)])


def far_swap(value):
    count = lax.axis_size(DOM)
    pairs = []
    for device in range(1, count, 2):
        after = (device + 1) % count
        pairs += [(device, after), (after, device)]
    return lax.ppermute(value, DOM, pairs)


def by_chip(value):
    return lax.all_to_all(value, CHIPS, 0, 0, tiled=True)


def local(
    residual_in,
    local_inverse,
    coarse_basis,
    coarse_inverse,
    multiplicity,
    iface_len,
    iface_dof,
    coarse_map,
):
    subs, cases, length = residual_in.shape
    coarse = coarse_basis.shape[1]
    width = iface_dof.shape[1]
    rows, order = coarse_inverse.shape
    chips = lax.axis_size(DOM) // 2
    half = cases // 2
    entries = subs * coarse
    spots = subs * width
    owned = spots // 2
    place = jnp.stack([lax.axis_index(DOM), lax.axis_index("c")]).astype(jnp.int32)
    core = place[1:]
    own_map = coarse_map.reshape(1, entries)
    slot_flops = 2 * 3 * cases * spots * spots
    sent = cases + coarse + 16
    blocks = f32(chips, half, order // chips)

    def buffers(count):
        return [
            pltpu.VMEM((subs, length, count), jnp.bfloat16),
            pltpu.SemaphoreType.DMA((subs,)),
        ]

    mate_map = swap(own_map)
    scaled, keep, send = call(
        first_kernel,
        "first",
        (bf16(subs, cases, length), f32(half, entries), f32(half, entries)),
        (core, residual_in, multiplicity, coarse_basis),
        [SMEM, VMEM, VMEM, VMEM],
        mib=60,
        scratch_shapes=[pltpu.VMEM((subs, entries, length), jnp.bfloat16)],
    )
    got = swap(send)
    other_rows = swap(coarse_inverse)

    def dense(keep, got, *after):
        parts = call(
            dense_kernel,
            "dense",
            blocks,
            (own_map, mate_map, keep, got, *after),
            [VMEM] * 4 + [ANY] * len(after),
        )
        return by_chip(parts)

    def local_solve(scaled, *more):
        specs = [SMEM] * 2 + [VMEM] * 3 + [HBM] + [VMEM] * len(more)
        rows = sent if more else cases
        outs = [bf16(entries, spots)] if more else []
        outs += [f32(cases, spots), f32(rows, owned), f32(rows, owned)]
        *own_basis, edge, mate, far = call(
            edge_kernel,
            "edge",
            tuple(outs),
            (place, iface_len, scaled, multiplicity, iface_dof, local_inverse, *more),
            specs,
            flops=slot_flops,
            moved=local_inverse.size // 2,
            mib=50,
            scratch_shapes=buffers(width),
        )
        from_far, from_mate = far_swap(far), swap(mate)
        inner = call(
            inner_kernel,
            "inner",
            f32(subs, cases, length - width),
            (scaled, local_inverse, mate, far),
            [VMEM, HBM, ANY, ANY],
            flops=2 * scaled.size * (length - width),
            moved=local_inverse.size * 3 // 2,
            mib=50,
            scratch_shapes=buffers(length - width),
        )
        return inner, edge, mate, far, from_mate, from_far, own_basis

    def coarse_solve(parts, after):
        rhs = call(
            sum_kernel, "sum", blocks, (parts, *after), [VMEM] + [ANY] * len(after)
        )
        rhs = by_chip(rhs)
        own = call(
            solve_kernel,
            "solve",
            blocks,
            (core, rhs, coarse_inverse, other_rows),
            [SMEM] + [VMEM] * 3,
        )
        return by_chip(own)

    def assemble(edge, mate, far, from_mate, from_far, after):
        return call(
            head_kernel,
            "head",
            f32(cases, spots),
            (place, iface_len, edge, mate, far, from_mate, from_far, iface_dof, after),
            [SMEM] * 2 + [VMEM] * 6 + [ANY],
            flops=slot_flops,
        )

    def correct(mine, head, shared, inner, *more):
        specs = [SMEM] + [VMEM] * 7 + [HBM] * 2 + [VMEM] * len(more)
        outs, out_specs = [f32(subs, cases, length)], [HBM]
        if more:
            outs += [bf16(subs, cases, length), f32(half, entries), f32(half, entries)]
            out_specs += [VMEM] * 3
        return call(
            correct_kernel,
            "correct",
            tuple(outs),
            (
                core,
                own_map,
                mate_map,
                far_map,
                mine,
                swap(mine),
                coarse_basis,
                head,
                shared,
                inner,
                *more,
            ),
            specs,
            out_specs=tuple(out_specs),
            scratch_shapes=[
                pltpu.VMEM((subs, entries, length), jnp.bfloat16),
                pltpu.VMEM((3 * entries, spots), jnp.bfloat16),
                pltpu.VMEM((subs, cases, length - width), jnp.float32),
                pltpu.VMEM((subs, cases, length), jnp.float32),
                pltpu.SemaphoreType.DMA((2 + subs,)),
            ],
        )

    inner, *arrays, from_mate, from_far, (own_basis,) = local_solve(scaled, coarse_basis, own_map)
    parts = dense(keep, got, inner, from_far, from_mate)
    head = assemble(*arrays, from_mate, from_far, parts)
    shared, far_map = call(
        share_kernel,
        "share",
        (bf16(3 * entries, spots), jax.ShapeDtypeStruct((1, entries), jnp.int32)),
        (place, iface_len, own_basis, from_mate, from_far, iface_dof, coarse_basis, parts),
        [SMEM] * 2 + [VMEM] * 5 + [ANY],
        flops=2 * 2 * entries * spots * spots,
        scratch_shapes=[pltpu.VMEM((2 * entries, owned), jnp.bfloat16)] * 2,
    )
    mine = coarse_solve(parts, (head, shared))
    first_apply, scaled, keep, send = correct(mine, head, shared, inner, multiplicity)

    inner, *arrays, from_mate, from_far, _ = local_solve(scaled)
    parts = dense(keep, swap(send), inner, from_far, from_mate)
    head = assemble(*arrays, from_mate, from_far, parts)
    mine = coarse_solve(parts, (head,))
    (second_apply,) = correct(mine, head, shared, inner)
    return first_apply, second_apply


def solution(mesh):
    grid = Mesh(mesh.devices.reshape(4, 4, 4, 2), DOM)
    placed = (
        P(DOM, None, None),
        P(DOM, None, None),
        P(DOM, None, None),
        P(DOM, None),
        P(DOM, None),
        P(DOM),
        P(DOM, None),
        P(DOM, None),
    )
    return jax.shard_map(
        local,
        mesh=grid,
        in_specs=placed,
        out_specs=(P(DOM, None, None), P(DOM, None, None)),
        check_vma=False,
    )
```

```python
import jax
import jax.numpy as jnp
from jax import lax
from jax.experimental import pallas as pl
from jax.experimental.pallas import tpu as pltpu
from jax.sharding import Mesh
from jax.sharding import PartitionSpec as P

CHIPS = ("y", "z", "x")
DOM = ("y", "z", "x", "c")
MIB = 2**20
VMEM = pl.BlockSpec(memory_space=pltpu.VMEM)
SMEM = pl.BlockSpec(memory_space=pltpu.SMEM)
ANY = pl.BlockSpec(memory_space=pl.ANY)
HBM = pl.BlockSpec(memory_space=pltpu.HBM)
BY_ROW = (((1,), (1,)), ((), ()))


def halves(value):
    high = value.astype(jnp.bfloat16)
    low = (value - high.astype(jnp.float32)).astype(jnp.bfloat16)
    return jnp.concatenate([high, low], axis=0)


def thirds(value):
    high = value.astype(jnp.bfloat16)
    rest = value - high.astype(jnp.float32)
    middle = rest.astype(jnp.bfloat16)
    low = (rest - middle.astype(jnp.float32)).astype(jnp.bfloat16)
    return jnp.concatenate([high, middle, low], axis=0)


def folded(out, rows):
    total = out[:rows]
    for start in range(rows, out.shape[0], rows):
        total = total + out[start : start + rows]
    return total


def mul(left, right):
    return jnp.dot(left, right, preferred_element_type=jnp.float32)


def mul_rows(left, right):
    return lax.dot_general(left, right, BY_ROW, preferred_element_type=jnp.float32)


def call(kernel, name, out_shape, args, specs, flops=1e6, moved=MIB, mib=16, **more):
    return pl.pallas_call(
        kernel,
        out_shape=out_shape,
        in_specs=specs,
        compiler_params=pltpu.CompilerParams(vmem_limit_bytes=mib * MIB),
        cost_estimate=pl.CostEstimate(
            flops=int(flops), bytes_accessed=int(moved), transcendentals=0
        ),
        name=name,
        **more,
    )(*args)


def f32(*shape):
    return jax.ShapeDtypeStruct(shape, jnp.float32)


def bf16(*shape):
    return jax.ShapeDtypeStruct(shape, jnp.bfloat16)


def weights_of(multiplicity):
    return 1.0 / multiplicity.astype(jnp.float32)


def part_out(place_ref, scaled_ref, basis_ref, keep_ref, send_ref):
    parts = mul_rows(scaled_ref[0], basis_ref[0])
    for sub in range(1, basis_ref.shape[0]):
        parts = parts + mul_rows(scaled_ref[sub], basis_ref[sub])
    half = keep_ref.shape[0]
    first = place_ref[1] == 0
    keep_ref[...] = jnp.where(first, parts[:half], parts[half:])
    send_ref[...] = jnp.where(first, parts[half:], parts[:half])


def widen(basis_ref, wide_ref):
    subs, coarse, _ = basis_ref.shape
    for sub in range(subs):
        wide_ref[sub] = jnp.zeros_like(wide_ref[sub])
        wide_ref[sub, sub * coarse : (sub + 1) * coarse] = basis_ref[sub]


def flat_map(map_ref):
    subs, coarse = map_ref.shape
    entries = subs * coarse
    value = map_ref[...]
    digits = jnp.concatenate([lax.div(value, 128), lax.rem(value, 128)], axis=0)
    lane = lax.broadcasted_iota(jnp.int32, (coarse, entries), 1)
    row = lax.broadcasted_iota(jnp.int32, (coarse, entries), 0)
    spread = jnp.where(lax.rem(lane, coarse) == row, 1.0, 0.0).astype(jnp.bfloat16)
    digits = mul(digits.astype(jnp.float32).astype(jnp.bfloat16), spread)
    value = digits[:subs] * 128.0 + digits[subs:]
    lane = lax.broadcasted_iota(jnp.int32, (subs, entries), 1)
    row = lax.broadcasted_iota(jnp.int32, (subs, entries), 0)
    own = jnp.where(lax.div(lane, coarse) == row, value, 0.0)
    return jnp.sum(own, axis=0, keepdims=True)


def hot_pair(maps, pair):
    rows = lax.broadcasted_iota(jnp.int32, (256, maps.shape[1]), 0) + 256 * pair
    return jnp.where(rows.astype(jnp.float32) == maps, 1.0, 0.0).astype(jnp.bfloat16)


def columns_of(rows):
    if rows.shape[0] == 1:
        rows = jnp.broadcast_to(rows, (8, rows.shape[1]))
    return rows.astype(jnp.float32).T


def dense_kernel(own_ref, mate_ref, keep_ref, got_ref, *refs):
    out_ref = refs[-1]
    cases, width = keep_ref.shape
    value = halves(jnp.concatenate([keep_ref[...], got_ref[...]], axis=1))
    maps = jnp.concatenate([flat_map(own_ref), flat_map(mate_ref)], axis=1)
    maps = columns_of(maps)[:, :1]
    wide = 2 * out_ref.shape[2]
    for pair in range(out_ref.shape[0] // 2):
        numbers = lax.broadcasted_iota(jnp.int32, (maps.shape[0], wide), 1) + wide * pair
        hot = jnp.where(numbers.astype(jnp.float32) == maps, 1.0, 0.0).astype(jnp.bfloat16)
        part = folded(mul(value, hot), cases)
        out_ref[2 * pair] = part[:, : wide // 2]
        out_ref[2 * pair + 1] = part[:, wide // 2 :]


def sum_kernel(parts_ref, *refs):
    out_ref = refs[-1]
    total = parts_ref[0]
    for chip in range(1, parts_ref.shape[0]):
        total = total + parts_ref[chip]
    for chip in range(out_ref.shape[0]):
        out_ref[chip] = total


def solve_kernel(core_ref, rhs_ref, mine_ref, other_ref, out_ref):
    cases, width = rhs_ref.shape[1:]
    total = jnp.zeros((2 * cases, 4 * mine_ref.shape[0]), jnp.float32)
    for pair in range(rhs_ref.shape[0] // 2):
        value = jnp.concatenate([rhs_ref[2 * pair], rhs_ref[2 * pair + 1]], axis=1)
        columns = slice(2 * pair * width, 2 * (pair + 1) * width)
        rows = jnp.concatenate([mine_ref[:, columns], other_ref[:, columns]], axis=0)
        total = total + mul_rows(halves(value), halves(rows))
    total = folded(total, cases)
    own = total[:, :width] + total[:, width:]
    half = width // 2
    turned = jnp.concatenate([own[:, half:], own[:, :half]], axis=1)
    own = jnp.where(core_ref[0] == 0, own, turned)
    for chip in range(out_ref.shape[0]):
        out_ref[chip] = own


def live_of(len_ref, sub, width):
    return lax.broadcasted_iota(jnp.int32, (1, width), 1) < len_ref[sub]


def slot_row(place_ref, len_ref, dof_ref, sub, spots):
    owned = spots // 2
    dof = dof_ref[sub : sub + 1]
    owner = lax.div(dof, owned)
    away = (owner != place_ref[0]).astype(jnp.int32)
    far = jnp.where(place_ref[1] == 0, away, 1 - away)
    live = live_of(len_ref, sub, dof.shape[1])
    return jnp.where(live, far * owned + (dof - owner * owned), -1)


def slots_of(place_ref, len_ref, dof_ref, sub, spots):
    slot = slot_row(place_ref, len_ref, dof_ref, sub, spots)
    rows = lax.broadcasted_iota(jnp.int32, (spots, slot.shape[1]), 0)
    return jnp.where(rows == slot, 1.0, 0.0).astype(jnp.bfloat16)


def column_copies(inverse_ref, buffer_ref, sems, start):
    copies = []
    for sub in range(inverse_ref.shape[0]):
        columns = pl.ds(start, buffer_ref.shape[2])
        copies.append(
            pltpu.make_async_copy(
                inverse_ref.at[sub, :, columns], buffer_ref.at[sub], sems.at[sub]
            )
        )
    for copy in copies:
        copy.start()
    return copies


def interface(len_ref, mult_ref, sub, width):
    live = live_of(len_ref, sub, width)
    return live, jnp.where(live, weights_of(mult_ref[sub : sub + 1, :width]), 0.0)


def slot_sums(
    place_ref, len_ref, mult_ref, dof_ref, start, edge_ref, sums_ref, basis_ref, map_ref, own_ref
):
    subs, width = dof_ref.shape
    owned = sums_ref.shape[1]
    slots = [slot_row(place_ref, len_ref, dof_ref, sub, 2 * owned) for sub in range(subs)]
    slots = columns_of(jnp.concatenate(slots, axis=0))
    numbers = lax.broadcasted_iota(jnp.int32, (width, owned), 1) + start
    numbers = numbers.astype(jnp.float32)
    total = None
    for sub in range(subs):
        live, mask = interface(len_ref, mult_ref, sub, width)
        hot = jnp.where(numbers == slots[:, sub : sub + 1], 1.0, 0.0).astype(jnp.bfloat16)
        solved = edge_ref[:, sub * width : (sub + 1) * width]
        cases = solved.shape[0]
        pieces = [thirds(solved * mask)]
        if basis_ref is not None:
            coarse = basis_ref.shape[1]
            weighted = basis_ref[sub, :, :width].astype(jnp.float32) * mask
            pieces.append(weighted.astype(jnp.bfloat16))
            number = jnp.where(live, float(sub), 0.0).astype(jnp.bfloat16)
            pieces.append(jnp.broadcast_to(number, (16, width)))
        out = mul(jnp.concatenate(pieces, axis=0), hot)
        moved = folded(out[: 3 * cases], cases)
        if basis_ref is not None:
            rest = out[3 * cases : 3 * cases + coarse + 8]
            own_ref[sub * coarse : (sub + 1) * coarse, :] = rest[:coarse].astype(jnp.bfloat16)
            moved = jnp.concatenate([moved, rest], axis=0)
        total = moved if total is None else total + moved
    count = total.shape[0]
    sums_ref[:count] = total
    if basis_ref is not None:
        flat = flat_map(map_ref)
        sums_ref[count:] = jnp.zeros_like(sums_ref[count:])
        sums_ref[count : count + 1, : flat.shape[1]] = flat


def edge_far(
    copies, place_ref, len_ref, mult_ref, dof_ref, scaled_ref, columns_ref, edge_ref, far_ref, *more
):
    subs, width = dof_ref.shape
    for copy in copies:
        copy.wait()
    solved = [mul(scaled_ref[sub], columns_ref[sub]) for sub in range(subs)]
    for sub in range(subs):
        edge_ref[:, sub * width : (sub + 1) * width] = solved[sub]
    start = far_ref.shape[1]
    slot_sums(place_ref, len_ref, mult_ref, dof_ref, start, edge_ref, far_ref, *more)


def first_kernel(
    place_ref,
    len_ref,
    values_hbm,
    mult_hbm,
    dof_hbm,
    map_hbm,
    basis_hbm,
    inverse_hbm,
    scaled_ref,
    keep_ref,
    send_ref,
    edge_ref,
    far_ref,
    own_ref,
    values_ref,
    mult_ref,
    dof_ref,
    map_ref,
    basis_ref,
    wide_ref,
    columns_ref,
    small_sems,
    sems,
):
    pairs = (
        (basis_hbm, basis_ref),
        (mult_hbm, mult_ref),
        (values_hbm, values_ref),
        (dof_hbm, dof_ref),
        (map_hbm, map_ref),
    )
    small = [
        pltpu.make_async_copy(source, target, small_sems.at[place])
        for place, (source, target) in enumerate(pairs)
    ]
    for copy in small:
        copy.start()
    copies = column_copies(inverse_hbm, columns_ref, sems, 0)
    subs, coarse, _ = basis_ref.shape
    for sub in range(subs):
        wide_ref[sub] = jnp.zeros_like(wide_ref[sub])
    for copy in small:
        copy.wait()
    for sub in range(subs):
        wide_ref[sub, sub * coarse : (sub + 1) * coarse] = basis_ref[sub]
        scaled = values_ref[sub].astype(jnp.float32) * weights_of(mult_ref[sub : sub + 1])
        scaled_ref[sub] = scaled.astype(jnp.bfloat16)
    part_out(place_ref, scaled_ref, wide_ref, keep_ref, send_ref)
    edge_far(
        copies,
        place_ref,
        len_ref,
        mult_ref,
        dof_ref,
        scaled_ref,
        columns_ref,
        edge_ref,
        far_ref,
        basis_ref,
        map_ref,
        own_ref,
    )


def inner_kernel(place_ref, len_ref, scaled_ref, mult_ref, dof_ref, edge_ref, inverse_ref, *refs):
    *inputs, buffer_ref, sems = refs
    if len(inputs) == 6:
        basis_ref, map_ref, after_ref, inner_ref, mate_ref, own_ref = inputs
    else:
        (after_ref, inner_ref, mate_ref), basis_ref, map_ref, own_ref = inputs, None, None, None
    copies = column_copies(
        inverse_ref, buffer_ref, sems, inverse_ref.shape[2] - buffer_ref.shape[2]
    )
    slot_sums(
        place_ref,
        len_ref,
        mult_ref,
        dof_ref,
        0,
        edge_ref,
        mate_ref,
        basis_ref,
        map_ref,
        own_ref,
    )
    for sub in range(scaled_ref.shape[0]):
        copies[sub].wait()
        inner_ref[sub] = mul(scaled_ref[sub], buffer_ref[sub])


def head_kernel(
    place_ref,
    len_ref,
    edge_ref,
    mate_ref,
    far_ref,
    from_mate_ref,
    from_far_ref,
    dof_ref,
    after_ref,
    *refs,
):
    subs, width = dof_ref.shape
    cases = edge_ref.shape[0]
    owned = mate_ref.shape[1]
    near = thirds(mate_ref[:cases] + from_mate_ref[:cases])
    far = thirds(far_ref[:cases] + from_far_ref[:cases])
    count = near.shape[0]
    if len(refs) == 1:
        (head_ref,) = refs
    else:
        basis_ref, own_mate_ref, own_far_ref, head_ref, shared_ref, map_ref, near_ref, wide_ref = refs
        coarse = basis_ref.shape[1]
        entries = own_mate_ref.shape[0]
        for ref, sums, own, arrived in (
            (near_ref, near, own_mate_ref, from_mate_ref),
            (wide_ref, far, own_far_ref, from_far_ref),
        ):
            ref[:count] = sums
            ref[count : count + entries] = own[...]
            row = arrived[cases + coarse : cases + coarse + 1]
            basis = arrived[cases : cases + coarse]
            for sub in range(subs):
                start = count + entries + sub * coarse
                ref[start : start + coarse] = jnp.where(row == float(sub), basis, 0.0).astype(
                    jnp.bfloat16
                )
        near, far = near_ref[...], wide_ref[...]
        map_ref[...] = from_far_ref[cases + coarse + 8 : cases + coarse + 9, :entries]
    for sub in range(subs):
        columns = slice(sub * width, (sub + 1) * width)
        hot = slots_of(place_ref, len_ref, dof_ref, sub, 2 * owned)
        by_mate = mul(near, hot[:owned])
        by_far = mul(far, hot[owned:])
        live = live_of(len_ref, sub, width)
        fetched = folded(by_mate[:count] + by_far[:count], cases)
        head_ref[:, columns] = jnp.where(live, fetched, edge_ref[:, columns])
        if len(refs) > 1:
            by_mate, by_far = by_mate[count:], by_far[count:]
            own = by_mate[:entries] + by_far[:entries]
            full = jnp.concatenate([own, by_mate[entries:], by_far[entries:]], axis=0)
            shared_ref[:, columns] = full.astype(jnp.bfloat16)
            rows = slice(sub * coarse, (sub + 1) * coarse)
            dead = jnp.where(live, 0.0, basis_ref[sub, :, :width].astype(jnp.float32))
            shared_ref[rows, columns] = (own[rows] + dead).astype(jnp.bfloat16)


def correct_kernel(
    place_ref,
    own_ref,
    mate_ref,
    far_map_ref,
    mine_ref,
    other_ref,
    basis_ref,
    head_ref,
    shared_ref,
    inner_ref,
    *refs,
):
    *inputs, wide_ref, values_ref, leave_sems = refs
    if len(inputs) == 1:
        (out_hbm,) = inputs
    else:
        (
            len_ref,
            mult_ref,
            dof_ref,
            inverse_hbm,
            out_hbm,
            scaled_ref,
            keep_ref,
            send_ref,
            edge_ref,
            far_ref,
            columns_ref,
            sems,
        ) = inputs
        copies = column_copies(inverse_hbm, columns_ref, sems, 0)
    subs, cases, _ = values_ref.shape
    chips, half, _ = mine_ref.shape
    entries = far_map_ref.shape[1]
    width = head_ref.shape[1] // subs
    leave = [
        pltpu.make_async_copy(values_ref.at[sub], out_hbm.at[sub], leave_sems.at[sub])
        for sub in range(subs)
    ]
    widen(basis_ref, wide_ref)
    maps = jnp.concatenate([flat_map(own_ref), flat_map(mate_ref), far_map_ref[...]], axis=1)
    looked = jnp.zeros((4 * half, 3 * entries), jnp.float32)
    for pair in range(chips // 2):
        mine = jnp.concatenate([mine_ref[2 * pair], mine_ref[2 * pair + 1]], axis=1)
        other = jnp.concatenate([other_ref[2 * pair], other_ref[2 * pair + 1]], axis=1)
        both = halves(jnp.concatenate([mine, other], axis=0))
        looked = looked + mul(both, hot_pair(maps, pair))
    looked = folded(looked, cases)
    turned = jnp.concatenate([looked[half:], looked[:half]], axis=0)
    looked = jnp.where(place_ref[1] == 0, looked, turned)
    own = thirds(looked[:, :entries])
    looked = thirds(looked)
    for sub in range(subs):
        columns = slice(sub * width, (sub + 1) * width)
        values_ref[sub, :, :width] = head_ref[:, columns] + folded(
            mul(looked, shared_ref[:, columns]), cases
        )
        values_ref[sub, :, width:] = inner_ref[sub] + folded(
            mul(own, wide_ref[sub, :, width:]), cases
        )
        leave[sub].start()
    if len(inputs) > 1:
        for sub in range(subs):
            scaled = values_ref[sub] * weights_of(mult_ref[sub : sub + 1])
            scaled_ref[sub] = scaled.astype(jnp.bfloat16)
        part_out(place_ref, scaled_ref, wide_ref, keep_ref, send_ref)
        edge_far(
            copies,
            place_ref,
            len_ref,
            mult_ref,
            dof_ref,
            scaled_ref,
            columns_ref,
            edge_ref,
            far_ref,
            None,
            None,
            None,
        )
    for copy in leave:
        copy.wait()


def swap(value):
    return lax.ppermute(value, "c", [(0, 1), (1, 0)])


def far_swap(value):
    count = lax.axis_size(DOM)
    pairs = []
    for device in range(1, count, 2):
        after = (device + 1) % count
        pairs += [(device, after), (after, device)]
    return lax.ppermute(value, DOM, pairs)


def by_chip(value):
    return lax.all_to_all(value, CHIPS, 0, 0, tiled=True)


def local(
    residual_in,
    local_inverse,
    coarse_basis,
    coarse_inverse,
    multiplicity,
    iface_len,
    iface_dof,
    coarse_map,
):
    subs, cases, length = residual_in.shape
    coarse = coarse_basis.shape[1]
    width = iface_dof.shape[1]
    rows, order = coarse_inverse.shape
    chips = lax.axis_size(DOM) // 2
    half = cases // 2
    entries = subs * coarse
    spots = subs * width
    owned = spots // 2
    place = jnp.stack([lax.axis_index(DOM), lax.axis_index("c")]).astype(jnp.int32)
    core = place[1:]
    slot_flops = 2 * 3 * cases * spots * spots
    sent = cases + coarse + 16
    blocks = f32(chips, half, order // chips)
    inverse_bytes = 2 * local_inverse.size

    def buffers(count):
        return [
            pltpu.VMEM((subs, length, count), jnp.bfloat16),
            pltpu.SemaphoreType.DMA((subs,)),
        ]

    mate_map = swap(coarse_map)
    other_rows = swap(coarse_inverse)
    wide = pltpu.VMEM((subs, entries, length), jnp.bfloat16)
    opened = (bf16(subs, cases, length), f32(half, entries), f32(half, entries), f32(cases, spots))

    def dense(keep, got, *after):
        parts = call(
            dense_kernel,
            "dense",
            blocks,
            (coarse_map, mate_map, keep, got, *after),
            [VMEM] * 4 + [ANY] * len(after),
        )
        return by_chip(parts)

    def inner_solve(scaled, edge, far, *more):
        outs = [f32(subs, cases, length - width), f32(sent if more else cases, owned)]
        if more:
            outs.append(bf16(entries, owned))
        return call(
            inner_kernel,
            "inner",
            tuple(outs),
            (place, iface_len, scaled, multiplicity, iface_dof, edge, local_inverse, *more, far),
            [SMEM] * 2 + [VMEM] * 4 + [HBM] + [VMEM] * len(more) + [ANY],
            flops=2 * scaled.size * (length - width) + slot_flops // 2,
            moved=inverse_bytes * 3 // 4,
            mib=60 if more else 50,
            scratch_shapes=buffers(length - width),
        )

    def coarse_solve(parts, after):
        rhs = call(
            sum_kernel, "sum", blocks, (parts, *after), [VMEM] + [ANY] * len(after)
        )
        rhs = by_chip(rhs)
        own = call(
            solve_kernel,
            "solve",
            blocks,
            (core, rhs, coarse_inverse, other_rows),
            [SMEM] + [VMEM] * 3,
        )
        return by_chip(own)

    def assemble(edge, mate, far, from_mate, from_far, after, *more):
        outs, scratch = [f32(cases, spots)], []
        if more:
            outs += [bf16(3 * entries, spots), f32(1, entries)]
            scratch = [pltpu.VMEM((3 * cases + 2 * entries, owned), jnp.bfloat16)] * 2
        return call(
            head_kernel,
            "head",
            tuple(outs),
            (place, iface_len, edge, mate, far, from_mate, from_far, iface_dof, after, *more),
            [SMEM] * 2 + [VMEM] * 6 + [ANY] + [VMEM] * len(more),
            flops=slot_flops,
            scratch_shapes=scratch,
        )

    def correct(mine, head, shared, inner, *more):
        outs, out_specs, specs, scratch = [f32(subs, cases, length)], [HBM], [], []
        if more:
            outs += [*opened, f32(cases, owned)]
            out_specs += [VMEM] * 5
            specs = [SMEM, VMEM, VMEM, HBM]
            scratch = buffers(width)
        return call(
            correct_kernel,
            "correct",
            tuple(outs),
            (
                place,
                coarse_map,
                mate_map,
                far_map,
                mine,
                swap(mine),
                coarse_basis,
                head,
                shared,
                inner,
                *more,
            ),
            [SMEM] + [VMEM] * 9 + specs,
            mib=50 if more else 16,
            out_specs=tuple(out_specs),
            scratch_shapes=[
                *scratch,
                wide,
                pltpu.VMEM((subs, cases, length), jnp.float32),
                pltpu.SemaphoreType.DMA((subs,)),
            ],
        )

    scaled, keep, send, edge, far, own_far = call(
        first_kernel,
        "first",
        (*opened, f32(sent, owned), bf16(entries, owned)),
        (
            place,
            iface_len,
            residual_in,
            multiplicity,
            iface_dof,
            coarse_map,
            coarse_basis,
            local_inverse,
        ),
        [SMEM] * 2 + [HBM] * 6,
        mib=60,
        scratch_shapes=[
            pltpu.VMEM(residual_in.shape, jnp.bfloat16),
            pltpu.VMEM(multiplicity.shape, jnp.int32),
            pltpu.VMEM(iface_dof.shape, jnp.int32),
            pltpu.VMEM(coarse_map.shape, jnp.int32),
            pltpu.VMEM(coarse_basis.shape, jnp.bfloat16),
            wide,
            buffers(width)[0],
            pltpu.SemaphoreType.DMA((5,)),
            buffers(width)[1],
        ],
    )
    got, from_far = swap(send), far_swap(far)
    inner, mate, own_mate = inner_solve(scaled, edge, far, coarse_basis, coarse_map)
    from_mate = swap(mate)
    parts = dense(keep, got, from_mate, from_far)
    head, shared, far_map = assemble(
        edge, mate, far, from_mate, from_far, parts, coarse_basis, own_mate, own_far
    )
    mine = coarse_solve(parts, (head,))
    first_apply, scaled, keep, send, edge, far = correct(
        mine, head, shared, inner, iface_len, multiplicity, iface_dof, local_inverse
    )

    got, from_far = swap(send), far_swap(far)
    inner, mate = inner_solve(scaled, edge, far)
    from_mate = swap(mate)
    parts = dense(keep, got, from_mate, from_far)
    (head,) = assemble(edge, mate, far, from_mate, from_far, parts)
    mine = coarse_solve(parts, (head,))
    (second_apply,) = correct(mine, head, shared, inner)
    return first_apply, second_apply


def solution(mesh):
    grid = Mesh(mesh.devices.reshape(4, 4, 4, 2), DOM)
    placed = (
        P(DOM, None, None),
        P(DOM, None, None),
        P(DOM, None, None),
        P(DOM, None),
        P(DOM, None),
        P(DOM),
        P(DOM, None),
        P(DOM, None),
    )
    return jax.shard_map(
        local,
        mesh=grid,
        in_specs=placed,
        out_specs=(P(DOM, None, None), P(DOM, None, None)),
        check_vma=False,
    )
```

```python
import jax
import jax.numpy as jnp
from jax import lax
from jax.experimental import pallas as pl
from jax.experimental.pallas import tpu as pltpu
from jax.sharding import Mesh
from jax.sharding import PartitionSpec as P

CHIPS = ("y", "z", "x")
DOM = ("y", "z", "x", "c")
MIB = 2**20
VMEM = pl.BlockSpec(memory_space=pltpu.VMEM)
SMEM = pl.BlockSpec(memory_space=pltpu.SMEM)
ANY = pl.BlockSpec(memory_space=pl.ANY)
HBM = pl.BlockSpec(memory_space=pltpu.HBM)
BY_ROW = (((1,), (1,)), ((), ()))


def halves(value):
    high = value.astype(jnp.bfloat16)
    low = (value - high.astype(jnp.float32)).astype(jnp.bfloat16)
    return jnp.concatenate([high, low], axis=0)


def thirds(value):
    high = value.astype(jnp.bfloat16)
    rest = value - high.astype(jnp.float32)
    middle = rest.astype(jnp.bfloat16)
    low = (rest - middle.astype(jnp.float32)).astype(jnp.bfloat16)
    return jnp.concatenate([high, middle, low], axis=0)


def folded(out, rows):
    total = out[:rows]
    for start in range(rows, out.shape[0], rows):
        total = total + out[start : start + rows]
    return total


def mul(left, right):
    return jnp.dot(left, right, preferred_element_type=jnp.float32)


def mul_rows(left, right):
    return lax.dot_general(left, right, BY_ROW, preferred_element_type=jnp.float32)


def call(kernel, name, out_shape, args, specs, flops=1e6, moved=MIB, mib=16, **more):
    return pl.pallas_call(
        kernel,
        out_shape=out_shape,
        in_specs=specs,
        compiler_params=pltpu.CompilerParams(vmem_limit_bytes=mib * MIB),
        cost_estimate=pl.CostEstimate(
            flops=int(flops), bytes_accessed=int(moved), transcendentals=0
        ),
        name=name,
        **more,
    )(*args)


def f32(*shape):
    return jax.ShapeDtypeStruct(shape, jnp.float32)


def bf16(*shape):
    return jax.ShapeDtypeStruct(shape, jnp.bfloat16)


def weights_of(multiplicity):
    return 1.0 / multiplicity.astype(jnp.float32)


def part_out(place_ref, scaled_ref, basis_ref, keep_ref, send_ref):
    parts = mul_rows(scaled_ref[0], basis_ref[0])
    for sub in range(1, basis_ref.shape[0]):
        parts = parts + mul_rows(scaled_ref[sub], basis_ref[sub])
    half = keep_ref.shape[0]
    first = place_ref[1] == 0
    keep_ref[...] = jnp.where(first, parts[:half], parts[half:])
    send_ref[...] = jnp.where(first, parts[half:], parts[:half])


def widen(basis_ref, wide_ref):
    subs, coarse, _ = basis_ref.shape
    for sub in range(subs):
        wide_ref[sub] = jnp.zeros_like(wide_ref[sub])
        wide_ref[sub, sub * coarse : (sub + 1) * coarse] = basis_ref[sub]


def flat_map(map_ref):
    subs, coarse = map_ref.shape
    entries = subs * coarse
    value = map_ref[...]
    digits = jnp.concatenate([lax.div(value, 128), lax.rem(value, 128)], axis=0)
    lane = lax.broadcasted_iota(jnp.int32, (coarse, entries), 1)
    row = lax.broadcasted_iota(jnp.int32, (coarse, entries), 0)
    spread = jnp.where(lax.rem(lane, coarse) == row, 1.0, 0.0).astype(jnp.bfloat16)
    digits = mul(digits.astype(jnp.float32).astype(jnp.bfloat16), spread)
    value = digits[:subs] * 128.0 + digits[subs:]
    lane = lax.broadcasted_iota(jnp.int32, (subs, entries), 1)
    row = lax.broadcasted_iota(jnp.int32, (subs, entries), 0)
    own = jnp.where(lax.div(lane, coarse) == row, value, 0.0)
    return jnp.sum(own, axis=0, keepdims=True)


def hot_pair(maps, pair):
    rows = lax.broadcasted_iota(jnp.int32, (256, maps.shape[1]), 0) + 256 * pair
    return jnp.where(rows.astype(jnp.float32) == maps, 1.0, 0.0).astype(jnp.bfloat16)


def columns_of(rows):
    if rows.shape[0] == 1:
        rows = jnp.broadcast_to(rows, (8, rows.shape[1]))
    return rows.astype(jnp.float32).T


def dense_kernel(own_ref, mate_ref, keep_ref, got_ref, *refs):
    out_ref = refs[-1]
    cases, width = keep_ref.shape
    value = halves(jnp.concatenate([keep_ref[...], got_ref[...]], axis=1))
    maps = jnp.concatenate([flat_map(own_ref), flat_map(mate_ref)], axis=1)
    maps = columns_of(maps)[:, :1]
    wide = 2 * out_ref.shape[2]
    for pair in range(out_ref.shape[0] // 2):
        numbers = lax.broadcasted_iota(jnp.int32, (maps.shape[0], wide), 1) + wide * pair
        hot = jnp.where(numbers.astype(jnp.float32) == maps, 1.0, 0.0).astype(jnp.bfloat16)
        part = folded(mul(value, hot), cases)
        out_ref[2 * pair] = part[:, : wide // 2]
        out_ref[2 * pair + 1] = part[:, wide // 2 :]


def sum_kernel(parts_ref, *refs):
    out_ref = refs[-1]
    total = parts_ref[0]
    for chip in range(1, parts_ref.shape[0]):
        total = total + parts_ref[chip]
    for chip in range(out_ref.shape[0]):
        out_ref[chip] = total


def solve_kernel(core_ref, rhs_ref, mine_ref, other_ref, out_ref):
    cases, width = rhs_ref.shape[1:]
    total = jnp.zeros((2 * cases, 4 * mine_ref.shape[0]), jnp.float32)
    for pair in range(rhs_ref.shape[0] // 2):
        value = jnp.concatenate([rhs_ref[2 * pair], rhs_ref[2 * pair + 1]], axis=1)
        columns = slice(2 * pair * width, 2 * (pair + 1) * width)
        rows = jnp.concatenate([mine_ref[:, columns], other_ref[:, columns]], axis=0)
        total = total + mul_rows(halves(value), halves(rows))
    total = folded(total, cases)
    own = total[:, :width] + total[:, width:]
    half = width // 2
    turned = jnp.concatenate([own[:, half:], own[:, :half]], axis=1)
    own = jnp.where(core_ref[0] == 0, own, turned)
    for chip in range(out_ref.shape[0]):
        out_ref[chip] = own


def live_of(len_ref, sub, width):
    return lax.broadcasted_iota(jnp.int32, (1, width), 1) < len_ref[sub]


def slot_row(place_ref, len_ref, dof_ref, sub, spots):
    owned = spots // 2
    dof = dof_ref[sub : sub + 1]
    owner = lax.div(dof, owned)
    away = (owner != place_ref[0]).astype(jnp.int32)
    far = jnp.where(place_ref[1] == 0, away, 1 - away)
    live = live_of(len_ref, sub, dof.shape[1])
    return jnp.where(live, far * owned + (dof - owner * owned), -1)


def slots_of(place_ref, len_ref, dof_ref, sub, spots):
    slot = slot_row(place_ref, len_ref, dof_ref, sub, spots)
    rows = lax.broadcasted_iota(jnp.int32, (spots, slot.shape[1]), 0)
    return jnp.where(rows == slot, 1.0, 0.0).astype(jnp.bfloat16)


def started(place_ref):
    return place_ref[0] >= 0


def column_copies(inverse_ref, buffer_ref, sems, start):
    copies = []
    for sub in range(inverse_ref.shape[0]):
        columns = pl.ds(start, buffer_ref.shape[2])
        copies.append(
            pltpu.make_async_copy(
                inverse_ref.at[sub, :, columns], buffer_ref.at[sub], sems.at[sub]
            )
        )
    for copy in copies:
        copy.start()
    return copies


def interface(len_ref, mult_ref, sub, width):
    live = live_of(len_ref, sub, width)
    return live, jnp.where(live, weights_of(mult_ref[sub : sub + 1, :width]), 0.0)


def slot_sums(
    place_ref, len_ref, mult_ref, dof_ref, start, edge_ref, sums_ref, basis_ref, map_ref, own_ref
):
    subs, width = dof_ref.shape
    owned = sums_ref.shape[1]
    slots = [slot_row(place_ref, len_ref, dof_ref, sub, 2 * owned) for sub in range(subs)]
    slots = columns_of(jnp.concatenate(slots, axis=0))
    numbers = lax.broadcasted_iota(jnp.int32, (width, owned), 1) + start
    numbers = numbers.astype(jnp.float32)
    total = None
    for sub in range(subs):
        live, mask = interface(len_ref, mult_ref, sub, width)
        hot = jnp.where(numbers == slots[:, sub : sub + 1], 1.0, 0.0).astype(jnp.bfloat16)
        solved = edge_ref[:, sub * width : (sub + 1) * width]
        cases = solved.shape[0]
        pieces = [thirds(solved * mask)]
        if basis_ref is not None:
            coarse = basis_ref.shape[1]
            weighted = basis_ref[sub, :, :width].astype(jnp.float32) * mask
            pieces.append(weighted.astype(jnp.bfloat16))
            number = jnp.where(live, float(sub), 0.0).astype(jnp.bfloat16)
            pieces.append(jnp.broadcast_to(number, (16, width)))
        out = mul(jnp.concatenate(pieces, axis=0), hot)
        moved = folded(out[: 3 * cases], cases)
        if basis_ref is not None:
            rest = out[3 * cases : 3 * cases + coarse + 8]
            own_ref[sub * coarse : (sub + 1) * coarse, :] = rest[:coarse].astype(jnp.bfloat16)
            moved = jnp.concatenate([moved, rest], axis=0)
        total = moved if total is None else total + moved
    count = total.shape[0]
    sums_ref[:count] = total
    if basis_ref is not None:
        flat = flat_map(map_ref)
        sums_ref[count:] = jnp.zeros_like(sums_ref[count:])
        sums_ref[count : count + 1, : flat.shape[1]] = flat


def edge_far(
    copies, place_ref, len_ref, mult_ref, dof_ref, scaled_ref, columns_ref, edge_ref, far_ref, *more
):
    subs, width = dof_ref.shape
    for copy in copies:
        copy.wait()
    solved = [mul(scaled_ref[sub], columns_ref[sub]) for sub in range(subs)]
    for sub in range(subs):
        edge_ref[:, sub * width : (sub + 1) * width] = solved[sub]
    start = far_ref.shape[1]
    slot_sums(place_ref, len_ref, mult_ref, dof_ref, start, edge_ref, far_ref, *more)


def first_kernel(
    place_ref,
    len_ref,
    values_hbm,
    mult_hbm,
    dof_hbm,
    map_hbm,
    basis_hbm,
    inverse_hbm,
    scaled_ref,
    edge_ref,
    far_ref,
    own_ref,
    values_ref,
    mult_ref,
    dof_ref,
    map_ref,
    basis_ref,
    columns_ref,
    small_sems,
    sems,
):
    pairs = (
        (basis_hbm, basis_ref),
        (mult_hbm, mult_ref),
        (values_hbm, values_ref),
        (dof_hbm, dof_ref),
        (map_hbm, map_ref),
    )
    small = [
        pltpu.make_async_copy(source, target, small_sems.at[place])
        for place, (source, target) in enumerate(pairs)
    ]
    for copy in small:
        copy.start()
    copies = column_copies(inverse_hbm, columns_ref, sems, 0)

    @pl.when(started(place_ref))
    def _():
        for copy in small:
            copy.wait()
        for sub in range(values_ref.shape[0]):
            scaled = values_ref[sub].astype(jnp.float32) * weights_of(mult_ref[sub : sub + 1])
            scaled_ref[sub] = scaled.astype(jnp.bfloat16)
        edge_far(
            copies,
            place_ref,
            len_ref,
            mult_ref,
            dof_ref,
            scaled_ref,
            columns_ref,
            edge_ref,
            far_ref,
            basis_ref,
            map_ref,
            own_ref,
        )


def inner_kernel(
    place_ref,
    len_ref,
    scaled_ref,
    mult_ref,
    dof_ref,
    edge_ref,
    basis_ref,
    inverse_ref,
    *refs,
):
    *inputs, wide_ref, buffer_ref, sems = refs
    copies = column_copies(
        inverse_ref, buffer_ref, sems, inverse_ref.shape[2] - buffer_ref.shape[2]
    )
    if len(inputs) == 7:
        map_ref, after_ref, inner_ref, mate_ref, keep_ref, send_ref, own_ref = inputs
        more = (basis_ref, map_ref, own_ref)
    else:
        after_ref, inner_ref, mate_ref, keep_ref, send_ref = inputs
        more = (None, None, None)

    @pl.when(started(place_ref))
    def _():
        widen(basis_ref, wide_ref)
        part_out(place_ref, scaled_ref, wide_ref, keep_ref, send_ref)
        slot_sums(place_ref, len_ref, mult_ref, dof_ref, 0, edge_ref, mate_ref, *more)

    for sub in range(scaled_ref.shape[0]):
        copies[sub].wait()
        inner_ref[sub] = mul(scaled_ref[sub], buffer_ref[sub])


def head_kernel(
    place_ref,
    len_ref,
    edge_ref,
    mate_ref,
    far_ref,
    from_mate_ref,
    from_far_ref,
    dof_ref,
    after_ref,
    *refs,
):
    subs, width = dof_ref.shape
    cases = edge_ref.shape[0]
    owned = mate_ref.shape[1]
    near = thirds(mate_ref[:cases] + from_mate_ref[:cases])
    far = thirds(far_ref[:cases] + from_far_ref[:cases])
    count = near.shape[0]
    if len(refs) == 1:
        (head_ref,) = refs
    else:
        basis_ref, own_mate_ref, own_far_ref, head_ref, shared_ref, map_ref, near_ref, wide_ref = refs
        coarse = basis_ref.shape[1]
        entries = own_mate_ref.shape[0]
        for ref, sums, own, arrived in (
            (near_ref, near, own_mate_ref, from_mate_ref),
            (wide_ref, far, own_far_ref, from_far_ref),
        ):
            ref[:count] = sums
            ref[count : count + entries] = own[...]
            row = arrived[cases + coarse : cases + coarse + 1]
            basis = arrived[cases : cases + coarse]
            for sub in range(subs):
                start = count + entries + sub * coarse
                ref[start : start + coarse] = jnp.where(row == float(sub), basis, 0.0).astype(
                    jnp.bfloat16
                )
        near, far = near_ref[...], wide_ref[...]
        map_ref[...] = from_far_ref[cases + coarse + 8 : cases + coarse + 9, :entries]
    for sub in range(subs):
        columns = slice(sub * width, (sub + 1) * width)
        hot = slots_of(place_ref, len_ref, dof_ref, sub, 2 * owned)
        by_mate = mul(near, hot[:owned])
        by_far = mul(far, hot[owned:])
        live = live_of(len_ref, sub, width)
        fetched = folded(by_mate[:count] + by_far[:count], cases)
        head_ref[:, columns] = jnp.where(live, fetched, edge_ref[:, columns])
        if len(refs) > 1:
            by_mate, by_far = by_mate[count:], by_far[count:]
            own = by_mate[:entries] + by_far[:entries]
            full = jnp.concatenate([own, by_mate[entries:], by_far[entries:]], axis=0)
            shared_ref[:, columns] = full.astype(jnp.bfloat16)
            rows = slice(sub * coarse, (sub + 1) * coarse)
            dead = jnp.where(live, 0.0, basis_ref[sub, :, :width].astype(jnp.float32))
            shared_ref[rows, columns] = (own[rows] + dead).astype(jnp.bfloat16)


def correct_kernel(
    place_ref,
    own_ref,
    mate_ref,
    far_map_ref,
    mine_ref,
    other_ref,
    basis_ref,
    head_ref,
    shared_ref,
    inner_ref,
    *refs,
):
    *inputs, wide_ref, values_ref, leave_sems = refs
    if len(inputs) == 1:
        (out_hbm,) = inputs
    else:
        (
            len_ref,
            mult_ref,
            dof_ref,
            inverse_hbm,
            out_hbm,
            scaled_ref,
            edge_ref,
            far_ref,
            columns_ref,
            sems,
        ) = inputs
        copies = column_copies(inverse_hbm, columns_ref, sems, 0)
    subs, cases, _ = values_ref.shape
    chips, half, _ = mine_ref.shape
    entries = far_map_ref.shape[1]
    width = head_ref.shape[1] // subs
    leave = [
        pltpu.make_async_copy(values_ref.at[sub], out_hbm.at[sub], leave_sems.at[sub])
        for sub in range(subs)
    ]

    @pl.when(started(place_ref))
    def _():
        widen(basis_ref, wide_ref)
        maps = jnp.concatenate([flat_map(own_ref), flat_map(mate_ref), far_map_ref[...]], axis=1)
        looked = jnp.zeros((4 * half, 3 * entries), jnp.float32)
        for pair in range(chips // 2):
            mine = jnp.concatenate([mine_ref[2 * pair], mine_ref[2 * pair + 1]], axis=1)
            other = jnp.concatenate([other_ref[2 * pair], other_ref[2 * pair + 1]], axis=1)
            both = halves(jnp.concatenate([mine, other], axis=0))
            looked = looked + mul(both, hot_pair(maps, pair))
        looked = folded(looked, cases)
        turned = jnp.concatenate([looked[half:], looked[:half]], axis=0)
        looked = jnp.where(place_ref[1] == 0, looked, turned)
        own = thirds(looked[:, :entries])
        looked = thirds(looked)
        for sub in range(subs):
            columns = slice(sub * width, (sub + 1) * width)
            values_ref[sub, :, :width] = head_ref[:, columns] + folded(
                mul(looked, shared_ref[:, columns]), cases
            )
            values_ref[sub, :, width:] = inner_ref[sub] + folded(
                mul(own, wide_ref[sub, :, width:]), cases
            )
            leave[sub].start()
        if len(inputs) > 1:
            for sub in range(subs):
                scaled = values_ref[sub] * weights_of(mult_ref[sub : sub + 1])
                scaled_ref[sub] = scaled.astype(jnp.bfloat16)
            edge_far(
                copies,
                place_ref,
                len_ref,
                mult_ref,
                dof_ref,
                scaled_ref,
                columns_ref,
                edge_ref,
                far_ref,
                None,
                None,
                None,
            )

    for copy in leave:
        copy.wait()


def swap(value):
    return lax.ppermute(value, "c", [(0, 1), (1, 0)])


def far_swap(value):
    count = lax.axis_size(DOM)
    pairs = []
    for device in range(1, count, 2):
        after = (device + 1) % count
        pairs += [(device, after), (after, device)]
    return lax.ppermute(value, DOM, pairs)


def by_chip(value):
    return lax.all_to_all(value, CHIPS, 0, 0, tiled=True)


def local(
    residual_in,
    local_inverse,
    coarse_basis,
    coarse_inverse,
    multiplicity,
    iface_len,
    iface_dof,
    coarse_map,
):
    subs, cases, length = residual_in.shape
    coarse = coarse_basis.shape[1]
    width = iface_dof.shape[1]
    rows, order = coarse_inverse.shape
    chips = lax.axis_size(DOM) // 2
    half = cases // 2
    entries = subs * coarse
    spots = subs * width
    owned = spots // 2
    place = jnp.stack([lax.axis_index(DOM), lax.axis_index("c")]).astype(jnp.int32)
    core = place[1:]
    slot_flops = 2 * 3 * cases * spots * spots
    sent = cases + coarse + 16
    blocks = f32(chips, half, order // chips)
    inverse_bytes = 2 * local_inverse.size

    def buffers(count):
        return [
            pltpu.VMEM((subs, length, count), jnp.bfloat16),
            pltpu.SemaphoreType.DMA((subs,)),
        ]

    mate_map = swap(coarse_map)
    other_rows = swap(coarse_inverse)
    wide = pltpu.VMEM((subs, entries, length), jnp.bfloat16)
    opened = (bf16(subs, cases, length), f32(cases, spots))

    def dense(keep, got, *after):
        parts = call(
            dense_kernel,
            "dense",
            blocks,
            (coarse_map, mate_map, keep, got, *after),
            [VMEM] * 4 + [ANY] * len(after),
        )
        return by_chip(parts)

    def inner_solve(scaled, edge, far, *more):
        outs = [f32(subs, cases, length - width), f32(sent if more else cases, owned)]
        outs += [f32(half, entries)] * 2
        if more:
            outs.append(bf16(entries, owned))
        return call(
            inner_kernel,
            "inner",
            tuple(outs),
            (
                place,
                iface_len,
                scaled,
                multiplicity,
                iface_dof,
                edge,
                coarse_basis,
                local_inverse,
                *more,
                far,
            ),
            [SMEM] * 2 + [VMEM] * 5 + [HBM] + [VMEM] * len(more) + [ANY],
            flops=2 * scaled.size * (length - width) + slot_flops // 2,
            moved=inverse_bytes * 3 // 4,
            mib=60 if more else 50,
            scratch_shapes=[wide, *buffers(length - width)],
        )

    def coarse_solve(parts, after):
        rhs = call(
            sum_kernel, "sum", blocks, (parts, *after), [VMEM] + [ANY] * len(after)
        )
        rhs = by_chip(rhs)
        own = call(
            solve_kernel,
            "solve",
            blocks,
            (core, rhs, coarse_inverse, other_rows),
            [SMEM] + [VMEM] * 3,
        )
        return by_chip(own)

    def assemble(edge, mate, far, from_mate, from_far, after, *more):
        outs, scratch = [f32(cases, spots)], []
        if more:
            outs += [bf16(3 * entries, spots), f32(1, entries)]
            scratch = [pltpu.VMEM((3 * cases + 2 * entries, owned), jnp.bfloat16)] * 2
        return call(
            head_kernel,
            "head",
            tuple(outs),
            (place, iface_len, edge, mate, far, from_mate, from_far, iface_dof, after, *more),
            [SMEM] * 2 + [VMEM] * 6 + [ANY] + [VMEM] * len(more),
            flops=slot_flops,
            scratch_shapes=scratch,
        )

    def correct(mine, head, shared, inner, *more):
        outs, out_specs, specs, scratch = [f32(subs, cases, length)], [HBM], [], []
        if more:
            outs += [*opened, f32(cases, owned)]
            out_specs += [VMEM] * 3
            specs = [SMEM, VMEM, VMEM, HBM]
            scratch = buffers(width)
        return call(
            correct_kernel,
            "correct",
            tuple(outs),
            (
                place,
                coarse_map,
                mate_map,
                far_map,
                mine,
                swap(mine),
                coarse_basis,
                head,
                shared,
                inner,
                *more,
            ),
            [SMEM] + [VMEM] * 9 + specs,
            mib=50 if more else 16,
            out_specs=tuple(out_specs),
            scratch_shapes=[
                *scratch,
                wide,
                pltpu.VMEM((subs, cases, length), jnp.float32),
                pltpu.SemaphoreType.DMA((subs,)),
            ],
        )

    scaled, edge, far, own_far = call(
        first_kernel,
        "first",
        (*opened, f32(sent, owned), bf16(entries, owned)),
        (
            place,
            iface_len,
            residual_in,
            multiplicity,
            iface_dof,
            coarse_map,
            coarse_basis,
            local_inverse,
        ),
        [SMEM] * 2 + [HBM] * 6,
        mib=60,
        scratch_shapes=[
            pltpu.VMEM(residual_in.shape, jnp.bfloat16),
            pltpu.VMEM(multiplicity.shape, jnp.int32),
            pltpu.VMEM(iface_dof.shape, jnp.int32),
            pltpu.VMEM(coarse_map.shape, jnp.int32),
            pltpu.VMEM(coarse_basis.shape, jnp.bfloat16),
            buffers(width)[0],
            pltpu.SemaphoreType.DMA((5,)),
            buffers(width)[1],
        ],
    )
    from_far = far_swap(far)
    inner, mate, keep, send, own_mate = inner_solve(scaled, edge, far, coarse_map)
    got, from_mate = swap(send), swap(mate)
    parts = dense(keep, got, from_mate, from_far)
    head, shared, far_map = assemble(
        edge, mate, far, from_mate, from_far, parts, coarse_basis, own_mate, own_far
    )
    mine = coarse_solve(parts, (head,))
    first_apply, scaled, edge, far = correct(
        mine, head, shared, inner, iface_len, multiplicity, iface_dof, local_inverse
    )

    from_far = far_swap(far)
    inner, mate, keep, send = inner_solve(scaled, edge, far)
    got, from_mate = swap(send), swap(mate)
    parts = dense(keep, got, from_mate, from_far)
    (head,) = assemble(edge, mate, far, from_mate, from_far, parts)
    mine = coarse_solve(parts, (head,))
    (second_apply,) = correct(mine, head, shared, inner)
    return first_apply, second_apply


def solution(mesh):
    grid = Mesh(mesh.devices.reshape(4, 4, 4, 2), DOM)
    placed = (
        P(DOM, None, None),
        P(DOM, None, None),
        P(DOM, None, None),
        P(DOM, None),
        P(DOM, None),
        P(DOM),
        P(DOM, None),
        P(DOM, None),
    )
    return jax.shard_map(
        local,
        mesh=grid,
        in_specs=placed,
        out_specs=(P(DOM, None, None), P(DOM, None, None)),
        check_vma=False,
    )
```

```python
import jax
import jax.numpy as jnp
from jax import lax
from jax.experimental import pallas as pl
from jax.experimental.pallas import tpu as pltpu
from jax.sharding import Mesh
from jax.sharding import PartitionSpec as P

CHIPS = ("y", "z", "x")
DOM = ("y", "z", "x", "c")
MIB = 2**20
VMEM = pl.BlockSpec(memory_space=pltpu.VMEM)
SMEM = pl.BlockSpec(memory_space=pltpu.SMEM)
ANY = pl.BlockSpec(memory_space=pl.ANY)
HBM = pl.BlockSpec(memory_space=pltpu.HBM)
BY_ROW = (((1,), (1,)), ((), ()))


def halves(value):
    high = value.astype(jnp.bfloat16)
    low = (value - high.astype(jnp.float32)).astype(jnp.bfloat16)
    return jnp.concatenate([high, low], axis=0)


def thirds(value):
    high = value.astype(jnp.bfloat16)
    rest = value - high.astype(jnp.float32)
    middle = rest.astype(jnp.bfloat16)
    low = (rest - middle.astype(jnp.float32)).astype(jnp.bfloat16)
    return jnp.concatenate([high, middle, low], axis=0)


def folded(out, rows):
    total = out[:rows]
    for start in range(rows, out.shape[0], rows):
        total = total + out[start : start + rows]
    return total


def mul(left, right):
    return jnp.dot(left, right, preferred_element_type=jnp.float32)


def mul_rows(left, right):
    return lax.dot_general(left, right, BY_ROW, preferred_element_type=jnp.float32)


def call(kernel, name, out_shape, args, specs, flops=1e6, moved=MIB, mib=16, **more):
    return pl.pallas_call(
        kernel,
        out_shape=out_shape,
        in_specs=specs,
        compiler_params=pltpu.CompilerParams(vmem_limit_bytes=mib * MIB),
        cost_estimate=pl.CostEstimate(
            flops=int(flops), bytes_accessed=int(moved), transcendentals=0
        ),
        name=name,
        **more,
    )(*args)


def f32(*shape):
    return jax.ShapeDtypeStruct(shape, jnp.float32)


def bf16(*shape):
    return jax.ShapeDtypeStruct(shape, jnp.bfloat16)


def weights_of(multiplicity):
    return 1.0 / multiplicity.astype(jnp.float32)


def parts_of(place_ref, scaled_ref, basis_ref):
    parts = mul_rows(scaled_ref[0], basis_ref[0])
    for sub in range(1, basis_ref.shape[0]):
        parts = parts + mul_rows(scaled_ref[sub], basis_ref[sub])
    half = parts.shape[0] // 2
    first = lax.rem(place_ref[0], 2) == 0
    keep = jnp.where(first, parts[:half], parts[half:])
    return keep, jnp.where(first, parts[half:], parts[:half])


def widen(basis_ref, wide_ref):
    subs, coarse, _ = basis_ref.shape
    for sub in range(subs):
        wide_ref[sub] = jnp.zeros_like(wide_ref[sub])
        wide_ref[sub, sub * coarse : (sub + 1) * coarse] = basis_ref[sub]


def flat_map(map_ref):
    subs, coarse = map_ref.shape
    entries = subs * coarse
    value = map_ref[...]
    digits = jnp.concatenate([lax.div(value, 128), lax.rem(value, 128)], axis=0)
    lane = lax.broadcasted_iota(jnp.int32, (coarse, entries), 1)
    row = lax.broadcasted_iota(jnp.int32, (coarse, entries), 0)
    spread = jnp.where(lax.rem(lane, coarse) == row, 1.0, 0.0).astype(jnp.bfloat16)
    digits = mul(digits.astype(jnp.float32).astype(jnp.bfloat16), spread)
    value = digits[:subs] * 128.0 + digits[subs:]
    lane = lax.broadcasted_iota(jnp.int32, (subs, entries), 1)
    row = lax.broadcasted_iota(jnp.int32, (subs, entries), 0)
    own = jnp.where(lax.div(lane, coarse) == row, value, 0.0)
    return jnp.sum(own, axis=0, keepdims=True)


def hot_pair(maps, pair):
    rows = lax.broadcasted_iota(jnp.int32, (256, maps.shape[1]), 0) + 256 * pair
    return jnp.where(rows.astype(jnp.float32) == maps, 1.0, 0.0).astype(jnp.bfloat16)


def columns_of(rows):
    if rows.shape[0] == 1:
        rows = jnp.broadcast_to(rows, (8, rows.shape[1]))
    return rows.astype(jnp.float32).T


def dense_kernel(own_ref, mate_ref, keep_ref, arrived_ref, *refs):
    out_ref = refs[-1]
    cases, width = keep_ref.shape
    got = arrived_ref[arrived_ref.shape[0] - cases // 2 :, : 2 * width]
    got = jnp.concatenate([got[:, :width], got[:, width:]], axis=0)
    value = halves(jnp.concatenate([keep_ref[...], got], axis=1))
    maps = jnp.concatenate([flat_map(own_ref), flat_map(mate_ref)], axis=1)
    maps = columns_of(maps)[:, :1]
    wide = 2 * out_ref.shape[2]
    for pair in range(out_ref.shape[0] // 2):
        numbers = lax.broadcasted_iota(jnp.int32, (maps.shape[0], wide), 1) + wide * pair
        hot = jnp.where(numbers.astype(jnp.float32) == maps, 1.0, 0.0).astype(jnp.bfloat16)
        part = folded(mul(value, hot), cases)
        out_ref[2 * pair] = part[:, : wide // 2]
        out_ref[2 * pair + 1] = part[:, wide // 2 :]


def sum_kernel(parts_ref, *refs):
    out_ref = refs[-1]
    total = parts_ref[0]
    for chip in range(1, parts_ref.shape[0]):
        total = total + parts_ref[chip]
    for chip in range(out_ref.shape[0]):
        out_ref[chip] = total


def solve_kernel(place_ref, rhs_ref, mine_ref, other_ref, out_ref):
    cases, width = rhs_ref.shape[1:]
    total = jnp.zeros((2 * cases, 4 * mine_ref.shape[0]), jnp.float32)
    for pair in range(rhs_ref.shape[0] // 2):
        value = jnp.concatenate([rhs_ref[2 * pair], rhs_ref[2 * pair + 1]], axis=1)
        columns = slice(2 * pair * width, 2 * (pair + 1) * width)
        rows = jnp.concatenate([mine_ref[:, columns], other_ref[:, columns]], axis=0)
        total = total + mul_rows(halves(value), halves(rows))
    total = folded(total, cases)
    own = total[:, :width] + total[:, width:]
    half = width // 2
    turned = jnp.concatenate([own[:, half:], own[:, :half]], axis=1)
    own = jnp.where(lax.rem(place_ref[0], 2) == 0, own, turned)
    for chip in range(out_ref.shape[0]):
        out_ref[chip] = own


def live_of(len_ref, sub, width):
    return lax.broadcasted_iota(jnp.int32, (1, width), 1) < len_ref[sub]


def slot_row(place_ref, len_ref, dof_ref, sub, spots):
    owned = spots // 2
    dof = dof_ref[sub : sub + 1]
    owner = lax.div(dof, owned)
    away = (owner != place_ref[0]).astype(jnp.int32)
    far = jnp.where(lax.rem(place_ref[0], 2) == 0, away, 1 - away)
    live = live_of(len_ref, sub, dof.shape[1])
    return jnp.where(live, far * owned + (dof - owner * owned), -1)


def slots_of(place_ref, len_ref, dof_ref, sub, spots):
    slot = slot_row(place_ref, len_ref, dof_ref, sub, spots)
    rows = lax.broadcasted_iota(jnp.int32, (spots, slot.shape[1]), 0)
    return jnp.where(rows == slot, 1.0, 0.0).astype(jnp.bfloat16)


def started(place_ref):
    return place_ref[0] >= 0


def column_copies(inverse_ref, buffer_ref, sems, start):
    copies = []
    for sub in range(inverse_ref.shape[0]):
        columns = pl.ds(start, buffer_ref.shape[2])
        copies.append(
            pltpu.make_async_copy(
                inverse_ref.at[sub, :, columns], buffer_ref.at[sub], sems.at[sub]
            )
        )
    for copy in copies:
        copy.start()
    return copies


def interface(len_ref, mult_ref, sub, width):
    live = live_of(len_ref, sub, width)
    return live, jnp.where(live, weights_of(mult_ref[sub : sub + 1, :width]), 0.0)


def slot_sums(
    place_ref, len_ref, mult_ref, dof_ref, start, edge_ref, sums_ref, basis_ref, map_ref, own_ref
):
    subs, width = dof_ref.shape
    owned = sums_ref.shape[1]
    slots = [slot_row(place_ref, len_ref, dof_ref, sub, 2 * owned) for sub in range(subs)]
    slots = columns_of(jnp.concatenate(slots, axis=0))
    numbers = lax.broadcasted_iota(jnp.int32, (width, owned), 1) + start
    numbers = numbers.astype(jnp.float32)
    total = None
    for sub in range(subs):
        live, mask = interface(len_ref, mult_ref, sub, width)
        hot = jnp.where(numbers == slots[:, sub : sub + 1], 1.0, 0.0).astype(jnp.bfloat16)
        solved = edge_ref[:, sub * width : (sub + 1) * width]
        cases = solved.shape[0]
        pieces = [thirds(solved * mask)]
        if basis_ref is not None:
            coarse = basis_ref.shape[1]
            weighted = basis_ref[sub, :, :width].astype(jnp.float32) * mask
            pieces.append(weighted.astype(jnp.bfloat16))
            number = jnp.where(live, float(sub), 0.0).astype(jnp.bfloat16)
            pieces.append(jnp.broadcast_to(number, (16, width)))
        out = mul(jnp.concatenate(pieces, axis=0), hot)
        moved = folded(out[: 3 * cases], cases)
        if basis_ref is not None:
            rest = out[3 * cases : 3 * cases + coarse + 8]
            own_ref[sub * coarse : (sub + 1) * coarse, :] = rest[:coarse].astype(jnp.bfloat16)
            moved = jnp.concatenate([moved, rest], axis=0)
        total = moved if total is None else total + moved
    count = total.shape[0]
    sums_ref[:count] = total
    sums_ref[count:] = jnp.zeros_like(sums_ref[count:])
    if basis_ref is not None:
        flat = flat_map(map_ref)
        sums_ref[count : count + 1, : flat.shape[1]] = flat


def edge_far(
    copies, place_ref, len_ref, mult_ref, dof_ref, scaled_ref, columns_ref, edge_ref, far_ref, *more
):
    subs, width = dof_ref.shape
    for copy in copies:
        copy.wait()
    solved = [mul(scaled_ref[sub], columns_ref[sub]) for sub in range(subs)]
    for sub in range(subs):
        edge_ref[:, sub * width : (sub + 1) * width] = solved[sub]
    start = far_ref.shape[1]
    slot_sums(place_ref, len_ref, mult_ref, dof_ref, start, edge_ref, far_ref, *more)


def first_kernel(
    place_ref,
    len_ref,
    values_hbm,
    mult_hbm,
    dof_hbm,
    map_hbm,
    basis_hbm,
    inverse_hbm,
    scaled_ref,
    edge_ref,
    far_ref,
    own_ref,
    values_ref,
    mult_ref,
    dof_ref,
    map_ref,
    basis_ref,
    columns_ref,
    small_sems,
    sems,
):
    pairs = (
        (basis_hbm, basis_ref),
        (mult_hbm, mult_ref),
        (values_hbm, values_ref),
        (dof_hbm, dof_ref),
        (map_hbm, map_ref),
    )
    small = [
        pltpu.make_async_copy(source, target, small_sems.at[place])
        for place, (source, target) in enumerate(pairs)
    ]
    for copy in small:
        copy.start()
    copies = column_copies(inverse_hbm, columns_ref, sems, 0)

    @pl.when(started(place_ref))
    def _():
        for copy in small:
            copy.wait()
        for sub in range(values_ref.shape[0]):
            scaled = values_ref[sub].astype(jnp.float32) * weights_of(mult_ref[sub : sub + 1])
            scaled_ref[sub] = scaled.astype(jnp.bfloat16)
        edge_far(
            copies,
            place_ref,
            len_ref,
            mult_ref,
            dof_ref,
            scaled_ref,
            columns_ref,
            edge_ref,
            far_ref,
            basis_ref,
            map_ref,
            own_ref,
        )


def inner_kernel(
    place_ref,
    len_ref,
    scaled_ref,
    mult_ref,
    dof_ref,
    edge_ref,
    basis_ref,
    inverse_ref,
    *refs,
):
    *inputs, wide_ref, buffer_ref, sems = refs
    copies = column_copies(
        inverse_ref, buffer_ref, sems, inverse_ref.shape[2] - buffer_ref.shape[2]
    )
    if len(inputs) == 7:
        map_ref, after_ref, _, inner_ref, mate_ref, keep_ref, own_ref = inputs
        more = (basis_ref, map_ref, own_ref)
    else:
        after_ref, _, inner_ref, mate_ref, keep_ref = inputs
        more = (None, None, None)

    @pl.when(started(place_ref))
    def _():
        widen(basis_ref, wide_ref)
        keep, send = parts_of(place_ref, scaled_ref, wide_ref)
        half, entries = keep.shape
        keep_ref[...] = keep
        slot_sums(place_ref, len_ref, mult_ref, dof_ref, 0, edge_ref, mate_ref, *more)
        last = mate_ref.shape[0] - half // 2
        mate_ref[last:, :entries] = send[: half // 2]
        mate_ref[last:, entries : 2 * entries] = send[half // 2 :]

    for sub in range(scaled_ref.shape[0]):
        copies[sub].wait()
        inner_ref[sub] = mul(scaled_ref[sub], buffer_ref[sub])


def head_kernel(
    place_ref,
    len_ref,
    edge_ref,
    mate_ref,
    far_ref,
    from_mate_ref,
    from_far_ref,
    dof_ref,
    after_ref,
    *refs,
):
    subs, width = dof_ref.shape
    cases = edge_ref.shape[0]
    owned = mate_ref.shape[1]
    near = thirds(mate_ref[:cases] + from_mate_ref[:cases])
    far = thirds(far_ref[:cases] + from_far_ref[:cases])
    count = near.shape[0]
    if len(refs) == 1:
        (head_ref,) = refs
    else:
        basis_ref, own_mate_ref, own_far_ref, head_ref, shared_ref, map_ref, near_ref, wide_ref = refs
        coarse = basis_ref.shape[1]
        entries = own_mate_ref.shape[0]
        for ref, sums, own, arrived in (
            (near_ref, near, own_mate_ref, from_mate_ref),
            (wide_ref, far, own_far_ref, from_far_ref),
        ):
            ref[:count] = sums
            ref[count : count + entries] = own[...]
            row = arrived[cases + coarse : cases + coarse + 1]
            basis = arrived[cases : cases + coarse]
            for sub in range(subs):
                start = count + entries + sub * coarse
                ref[start : start + coarse] = jnp.where(row == float(sub), basis, 0.0).astype(
                    jnp.bfloat16
                )
        near, far = near_ref[...], wide_ref[...]
        map_ref[...] = from_far_ref[cases + coarse + 8 : cases + coarse + 9, :entries]
    for sub in range(subs):
        columns = slice(sub * width, (sub + 1) * width)
        hot = slots_of(place_ref, len_ref, dof_ref, sub, 2 * owned)
        by_mate = mul(near, hot[:owned])
        by_far = mul(far, hot[owned:])
        live = live_of(len_ref, sub, width)
        fetched = folded(by_mate[:count] + by_far[:count], cases)
        head_ref[:, columns] = jnp.where(live, fetched, edge_ref[:, columns])
        if len(refs) > 1:
            by_mate, by_far = by_mate[count:], by_far[count:]
            own = by_mate[:entries] + by_far[:entries]
            full = jnp.concatenate([own, by_mate[entries:], by_far[entries:]], axis=0)
            shared_ref[:, columns] = full.astype(jnp.bfloat16)
            rows = slice(sub * coarse, (sub + 1) * coarse)
            dead = jnp.where(live, 0.0, basis_ref[sub, :, :width].astype(jnp.float32))
            shared_ref[rows, columns] = (own[rows] + dead).astype(jnp.bfloat16)


def correct_kernel(
    place_ref,
    own_ref,
    mate_ref,
    far_map_ref,
    mine_ref,
    other_ref,
    basis_ref,
    head_ref,
    shared_ref,
    inner_ref,
    *refs,
):
    *inputs, wide_ref, values_ref, leave_sems = refs
    if len(inputs) == 1:
        (out_hbm,) = inputs
    else:
        (
            len_ref,
            mult_ref,
            dof_ref,
            inverse_hbm,
            out_hbm,
            scaled_ref,
            edge_ref,
            far_ref,
            columns_ref,
            sems,
        ) = inputs
        copies = column_copies(inverse_hbm, columns_ref, sems, 0)
    subs, cases, _ = values_ref.shape
    chips, half, _ = mine_ref.shape
    entries = far_map_ref.shape[1]
    width = head_ref.shape[1] // subs
    leave = [
        pltpu.make_async_copy(values_ref.at[sub], out_hbm.at[sub], leave_sems.at[sub])
        for sub in range(subs)
    ]

    @pl.when(started(place_ref))
    def _():
        widen(basis_ref, wide_ref)
        maps = jnp.concatenate([flat_map(own_ref), flat_map(mate_ref), far_map_ref[...]], axis=1)
        looked = jnp.zeros((4 * half, 3 * entries), jnp.float32)
        for pair in range(chips // 2):
            mine = jnp.concatenate([mine_ref[2 * pair], mine_ref[2 * pair + 1]], axis=1)
            other = jnp.concatenate([other_ref[2 * pair], other_ref[2 * pair + 1]], axis=1)
            both = halves(jnp.concatenate([mine, other], axis=0))
            looked = looked + mul(both, hot_pair(maps, pair))
        looked = folded(looked, cases)
        turned = jnp.concatenate([looked[half:], looked[:half]], axis=0)
        looked = jnp.where(lax.rem(place_ref[0], 2) == 0, looked, turned)
        own = thirds(looked[:, :entries])
        looked = thirds(looked)
        for sub in range(subs):
            columns = slice(sub * width, (sub + 1) * width)
            values_ref[sub, :, :width] = head_ref[:, columns] + folded(
                mul(looked, shared_ref[:, columns]), cases
            )
            values_ref[sub, :, width:] = inner_ref[sub] + folded(
                mul(own, wide_ref[sub, :, width:]), cases
            )
            leave[sub].start()
        if len(inputs) > 1:
            for sub in range(subs):
                scaled = values_ref[sub] * weights_of(mult_ref[sub : sub + 1])
                scaled_ref[sub] = scaled.astype(jnp.bfloat16)
            edge_far(
                copies,
                place_ref,
                len_ref,
                mult_ref,
                dof_ref,
                scaled_ref,
                columns_ref,
                edge_ref,
                far_ref,
                None,
                None,
                None,
            )

    for copy in leave:
        copy.wait()


def swap(value):
    return lax.ppermute(value, "c", [(0, 1), (1, 0)])


def far_swap(value):
    count = lax.axis_size(DOM)
    pairs = []
    for device in range(1, count, 2):
        after = (device + 1) % count
        pairs += [(device, after), (after, device)]
    return lax.ppermute(value, DOM, pairs)


def by_chip(value):
    return lax.all_to_all(value, CHIPS, 0, 0, tiled=True)


def local(
    residual_in,
    local_inverse,
    coarse_basis,
    coarse_inverse,
    multiplicity,
    iface_len,
    iface_dof,
    coarse_map,
):
    subs, cases, length = residual_in.shape
    coarse = coarse_basis.shape[1]
    width = iface_dof.shape[1]
    rows, order = coarse_inverse.shape
    chips = lax.axis_size(DOM) // 2
    half = cases // 2
    entries = subs * coarse
    spots = subs * width
    owned = spots // 2
    place = lax.axis_index(DOM).astype(jnp.int32).reshape(1)
    slot_flops = 2 * 3 * cases * spots * spots
    kept = cases + half // 2
    sent = kept + coarse + 16
    blocks = f32(chips, half, order // chips)
    inverse_bytes = 2 * local_inverse.size

    def buffers(count):
        return [
            pltpu.VMEM((subs, length, count), jnp.bfloat16),
            pltpu.SemaphoreType.DMA((subs,)),
        ]

    mate_map = swap(coarse_map)
    other_rows = swap(coarse_inverse)
    wide = pltpu.VMEM((subs, entries, length), jnp.bfloat16)
    opened = (bf16(subs, cases, length), f32(cases, spots))

    def dense(keep, arrived, *after):
        parts = call(
            dense_kernel,
            "dense",
            blocks,
            (coarse_map, mate_map, keep, arrived, *after),
            [VMEM] * 4 + [ANY] * len(after),
        )
        return by_chip(parts)

    def inner_solve(scaled, edge, far, *more):
        outs = [f32(subs, cases, length - width), f32(sent if more else kept, owned)]
        outs.append(f32(half, entries))
        if more:
            outs.append(bf16(entries, owned))
        return call(
            inner_kernel,
            "inner",
            tuple(outs),
            (
                place,
                iface_len,
                scaled,
                multiplicity,
                iface_dof,
                edge,
                coarse_basis,
                local_inverse,
                *more,
                far,
                mate_map,
            ),
            [SMEM] * 2 + [VMEM] * 5 + [HBM] + [VMEM] * len(more) + [ANY] * 2,
            flops=2 * scaled.size * (length - width) + slot_flops // 2,
            moved=inverse_bytes * 3 // 4,
            mib=60 if more else 50,
            scratch_shapes=[wide, *buffers(length - width)],
        )

    def coarse_solve(parts, after):
        rhs = call(
            sum_kernel, "sum", blocks, (parts, *after), [VMEM] + [ANY] * len(after)
        )
        rhs = by_chip(rhs)
        own = call(
            solve_kernel,
            "solve",
            blocks,
            (place, rhs, coarse_inverse, other_rows),
            [SMEM] + [VMEM] * 3,
        )
        return by_chip(own)

    def assemble(edge, mate, far, from_mate, from_far, after, *more):
        outs, scratch = [f32(cases, spots)], []
        if more:
            outs += [bf16(3 * entries, spots), f32(1, entries)]
            scratch = [pltpu.VMEM((3 * cases + 2 * entries, owned), jnp.bfloat16)] * 2
        return call(
            head_kernel,
            "head",
            tuple(outs),
            (place, iface_len, edge, mate, far, from_mate, from_far, iface_dof, after, *more),
            [SMEM] * 2 + [VMEM] * 6 + [ANY] + [VMEM] * len(more),
            flops=slot_flops,
            scratch_shapes=scratch,
        )

    def correct(mine, head, shared, inner, *more):
        outs, out_specs, specs, scratch = [f32(subs, cases, length)], [HBM], [], []
        if more:
            outs += [*opened, f32(kept, owned)]
            out_specs += [VMEM] * 3
            specs = [SMEM, VMEM, VMEM, HBM]
            scratch = buffers(width)
        return call(
            correct_kernel,
            "correct",
            tuple(outs),
            (
                place,
                coarse_map,
                mate_map,
                far_map,
                mine,
                swap(mine),
                coarse_basis,
                head,
                shared,
                inner,
                *more,
            ),
            [SMEM] + [VMEM] * 9 + specs,
            mib=50 if more else 16,
            out_specs=tuple(out_specs),
            scratch_shapes=[
                *scratch,
                wide,
                pltpu.VMEM((subs, cases, length), jnp.float32),
                pltpu.SemaphoreType.DMA((subs,)),
            ],
        )

    scaled, edge, far, own_far = call(
        first_kernel,
        "first",
        (*opened, f32(sent, owned), bf16(entries, owned)),
        (
            place,
            iface_len,
            residual_in,
            multiplicity,
            iface_dof,
            coarse_map,
            coarse_basis,
            local_inverse,
        ),
        [SMEM] * 2 + [HBM] * 6,
        mib=60,
        scratch_shapes=[
            pltpu.VMEM(residual_in.shape, jnp.bfloat16),
            pltpu.VMEM(multiplicity.shape, jnp.int32),
            pltpu.VMEM(iface_dof.shape, jnp.int32),
            pltpu.VMEM(coarse_map.shape, jnp.int32),
            pltpu.VMEM(coarse_basis.shape, jnp.bfloat16),
            buffers(width)[0],
            pltpu.SemaphoreType.DMA((5,)),
            buffers(width)[1],
        ],
    )
    from_far = far_swap(far)
    inner, mate, keep, own_mate = inner_solve(scaled, edge, far, coarse_map)
    from_mate = swap(mate)
    parts = dense(keep, from_mate, from_far)
    head, shared, far_map = assemble(
        edge, mate, far, from_mate, from_far, parts, coarse_basis, own_mate, own_far
    )
    mine = coarse_solve(parts, (head,))
    first_apply, scaled, edge, far = correct(
        mine, head, shared, inner, iface_len, multiplicity, iface_dof, local_inverse
    )

    from_far = far_swap(far)
    inner, mate, keep = inner_solve(scaled, edge, far)
    from_mate = swap(mate)
    parts = dense(keep, from_mate, from_far)
    (head,) = assemble(edge, mate, far, from_mate, from_far, parts)
    mine = coarse_solve(parts, (head,))
    (second_apply,) = correct(mine, head, shared, inner)
    return first_apply, second_apply


def solution(mesh):
    grid = Mesh(mesh.devices.reshape(4, 4, 4, 2), DOM)
    placed = (
        P(DOM, None, None),
        P(DOM, None, None),
        P(DOM, None, None),
        P(DOM, None),
        P(DOM, None),
        P(DOM),
        P(DOM, None),
        P(DOM, None),
    )
    return jax.shard_map(
        local,
        mesh=grid,
        in_specs=placed,
        out_specs=(P(DOM, None, None), P(DOM, None, None)),
        check_vma=False,
    )
```

```python
import functools

import jax
import jax.numpy as jnp
from jax import lax
from jax.experimental import pallas as pl
from jax.experimental.pallas import tpu as pltpu
from jax.sharding import Mesh
from jax.sharding import PartitionSpec as P

CHIPS = ("y", "z", "x")
DOM = ("y", "z", "x", "c")
MIB = 2**20
VMEM = pl.BlockSpec(memory_space=pltpu.VMEM)
SMEM = pl.BlockSpec(memory_space=pltpu.SMEM)
ANY = pl.BlockSpec(memory_space=pl.ANY)
HBM = pl.BlockSpec(memory_space=pltpu.HBM)
BY_ROW = (((1,), (1,)), ((), ()))


def halves(value):
    high = value.astype(jnp.bfloat16)
    low = (value - high.astype(jnp.float32)).astype(jnp.bfloat16)
    return jnp.concatenate([high, low], axis=0)


def thirds(value):
    high = value.astype(jnp.bfloat16)
    rest = value - high.astype(jnp.float32)
    middle = rest.astype(jnp.bfloat16)
    low = (rest - middle.astype(jnp.float32)).astype(jnp.bfloat16)
    return jnp.concatenate([high, middle, low], axis=0)


def folded(out, rows):
    total = out[:rows]
    for start in range(rows, out.shape[0], rows):
        total = total + out[start : start + rows]
    return total


def mul(left, right):
    return jnp.dot(left, right, preferred_element_type=jnp.float32)


def mul_rows(left, right):
    return lax.dot_general(left, right, BY_ROW, preferred_element_type=jnp.float32)


def call(kernel, name, out_shape, args, specs, flops=1e6, moved=MIB, mib=16, **more):
    return pl.pallas_call(
        kernel,
        out_shape=out_shape,
        in_specs=specs,
        compiler_params=pltpu.CompilerParams(vmem_limit_bytes=mib * MIB),
        cost_estimate=pl.CostEstimate(
            flops=int(flops), bytes_accessed=int(moved), transcendentals=0
        ),
        name=name,
        **more,
    )(*args)


def f32(*shape):
    return jax.ShapeDtypeStruct(shape, jnp.float32)


def bf16(*shape):
    return jax.ShapeDtypeStruct(shape, jnp.bfloat16)


def weights_of(multiplicity):
    return 1.0 / multiplicity.astype(jnp.float32)


def parts_of(place_ref, scaled_ref, basis_ref):
    parts = mul_rows(scaled_ref[0], basis_ref[0])
    for sub in range(1, basis_ref.shape[0]):
        parts = parts + mul_rows(scaled_ref[sub], basis_ref[sub])
    half = parts.shape[0] // 2
    first = lax.rem(place_ref[0], 2) == 0
    keep = jnp.where(first, parts[:half], parts[half:])
    return keep, jnp.where(first, parts[half:], parts[:half])


def widen(basis_ref, wide_ref):
    subs, coarse, _ = basis_ref.shape
    for sub in range(subs):
        wide_ref[sub] = jnp.zeros_like(wide_ref[sub])
        wide_ref[sub, sub * coarse : (sub + 1) * coarse] = basis_ref[sub]


def flat_map(map_ref):
    subs, coarse = map_ref.shape
    entries = subs * coarse
    value = map_ref[...]
    digits = jnp.concatenate([lax.div(value, 128), lax.rem(value, 128)], axis=0)
    lane = lax.broadcasted_iota(jnp.int32, (coarse, entries), 1)
    row = lax.broadcasted_iota(jnp.int32, (coarse, entries), 0)
    spread = jnp.where(lax.rem(lane, coarse) == row, 1.0, 0.0).astype(jnp.bfloat16)
    digits = mul(digits.astype(jnp.float32).astype(jnp.bfloat16), spread)
    value = digits[:subs] * 128.0 + digits[subs:]
    lane = lax.broadcasted_iota(jnp.int32, (subs, entries), 1)
    row = lax.broadcasted_iota(jnp.int32, (subs, entries), 0)
    own = jnp.where(lax.div(lane, coarse) == row, value, 0.0)
    return jnp.sum(own, axis=0, keepdims=True)


def hot_pair(maps, pair):
    rows = lax.broadcasted_iota(jnp.int32, (256, maps.shape[1]), 0) + 256 * pair
    return jnp.where(rows.astype(jnp.float32) == maps, 1.0, 0.0).astype(jnp.bfloat16)


def columns_of(rows):
    if rows.shape[0] == 1:
        rows = jnp.broadcast_to(rows, (8, rows.shape[1]))
    return rows.astype(jnp.float32).T


def dense_kernel(row, own_ref, near_ref, keep_ref, arrived_ref, *refs):
    out_ref = refs[-1]
    cases, width = keep_ref.shape
    got = arrived_ref[arrived_ref.shape[0] - cases // 2 :, : 2 * width]
    got = jnp.concatenate([got[:, :width], got[:, width:]], axis=0)
    value = halves(jnp.concatenate([keep_ref[...], got], axis=1))
    mate = near_ref[row : row + 1, :width]
    maps = jnp.concatenate([flat_map(own_ref), mate], axis=1)
    maps = columns_of(maps)[:, :1]
    wide = 2 * out_ref.shape[2]
    for pair in range(out_ref.shape[0] // 2):
        numbers = lax.broadcasted_iota(jnp.int32, (maps.shape[0], wide), 1) + wide * pair
        hot = jnp.where(numbers.astype(jnp.float32) == maps, 1.0, 0.0).astype(jnp.bfloat16)
        part = folded(mul(value, hot), cases)
        out_ref[2 * pair] = part[:, : wide // 2]
        out_ref[2 * pair + 1] = part[:, wide // 2 :]


def sum_kernel(parts_ref, *refs):
    out_ref = refs[-1]
    total = parts_ref[0]
    for chip in range(1, parts_ref.shape[0]):
        total = total + parts_ref[chip]
    for chip in range(out_ref.shape[0]):
        out_ref[chip] = total


def solve_kernel(place_ref, rhs_ref, mine_ref, other_ref, out_ref):
    cases, width = rhs_ref.shape[1:]
    total = jnp.zeros((2 * cases, 4 * mine_ref.shape[0]), jnp.float32)
    for pair in range(rhs_ref.shape[0] // 2):
        value = jnp.concatenate([rhs_ref[2 * pair], rhs_ref[2 * pair + 1]], axis=1)
        columns = slice(2 * pair * width, 2 * (pair + 1) * width)
        rows = jnp.concatenate([mine_ref[:, columns], other_ref[:, columns]], axis=0)
        total = total + mul_rows(halves(value), halves(rows))
    total = folded(total, cases)
    own = total[:, :width] + total[:, width:]
    half = width // 2
    turned = jnp.concatenate([own[:, half:], own[:, :half]], axis=1)
    own = jnp.where(lax.rem(place_ref[0], 2) == 0, own, turned)
    for chip in range(out_ref.shape[0]):
        out_ref[chip] = own


def live_of(len_ref, sub, width):
    return lax.broadcasted_iota(jnp.int32, (1, width), 1) < len_ref[sub]


def slot_row(place_ref, len_ref, dof_ref, sub, spots):
    owned = spots // 2
    dof = dof_ref[sub : sub + 1]
    owner = lax.div(dof, owned)
    away = (owner != place_ref[0]).astype(jnp.int32)
    far = jnp.where(lax.rem(place_ref[0], 2) == 0, away, 1 - away)
    live = live_of(len_ref, sub, dof.shape[1])
    return jnp.where(live, far * owned + (dof - owner * owned), -1)


def slots_of(place_ref, len_ref, dof_ref, sub, spots):
    slot = slot_row(place_ref, len_ref, dof_ref, sub, spots)
    rows = lax.broadcasted_iota(jnp.int32, (spots, slot.shape[1]), 0)
    return jnp.where(rows == slot, 1.0, 0.0).astype(jnp.bfloat16)


def started(place_ref):
    return place_ref[0] >= 0


def column_copies(inverse_ref, buffer_ref, sems, start):
    copies = []
    for sub in range(inverse_ref.shape[0]):
        columns = pl.ds(start, buffer_ref.shape[2])
        copies.append(
            pltpu.make_async_copy(
                inverse_ref.at[sub, :, columns], buffer_ref.at[sub], sems.at[sub]
            )
        )
    for copy in copies:
        copy.start()
    return copies


def interface(len_ref, mult_ref, sub, width):
    live = live_of(len_ref, sub, width)
    return live, jnp.where(live, weights_of(mult_ref[sub : sub + 1, :width]), 0.0)


def slot_sums(
    place_ref, len_ref, mult_ref, dof_ref, start, edge_ref, sums_ref, basis_ref, map_ref, own_ref
):
    subs, width = dof_ref.shape
    owned = sums_ref.shape[1]
    slots = [slot_row(place_ref, len_ref, dof_ref, sub, 2 * owned) for sub in range(subs)]
    slots = columns_of(jnp.concatenate(slots, axis=0))
    numbers = lax.broadcasted_iota(jnp.int32, (width, owned), 1) + start
    numbers = numbers.astype(jnp.float32)
    total = None
    for sub in range(subs):
        live, mask = interface(len_ref, mult_ref, sub, width)
        hot = jnp.where(numbers == slots[:, sub : sub + 1], 1.0, 0.0).astype(jnp.bfloat16)
        solved = edge_ref[:, sub * width : (sub + 1) * width]
        cases = solved.shape[0]
        pieces = [thirds(solved * mask)]
        if basis_ref is not None:
            coarse = basis_ref.shape[1]
            weighted = basis_ref[sub, :, :width].astype(jnp.float32) * mask
            pieces.append(weighted.astype(jnp.bfloat16))
            number = jnp.where(live, float(sub), 0.0).astype(jnp.bfloat16)
            pieces.append(jnp.broadcast_to(number, (16, width)))
        out = mul(jnp.concatenate(pieces, axis=0), hot)
        moved = folded(out[: 3 * cases], cases)
        if basis_ref is not None:
            rest = out[3 * cases : 3 * cases + coarse + 8]
            own_ref[sub * coarse : (sub + 1) * coarse, :] = rest[:coarse].astype(jnp.bfloat16)
            moved = jnp.concatenate([moved, rest], axis=0)
        total = moved if total is None else total + moved
    count = total.shape[0]
    sums_ref[:count] = total
    sums_ref[count:] = jnp.zeros_like(sums_ref[count:])
    if basis_ref is not None:
        flat = flat_map(map_ref)
        sums_ref[count : count + 1, : flat.shape[1]] = flat


def edge_far(
    copies, place_ref, len_ref, mult_ref, dof_ref, scaled_ref, columns_ref, edge_ref, far_ref, *more
):
    subs, width = dof_ref.shape
    for copy in copies:
        copy.wait()
    solved = [mul(scaled_ref[sub], columns_ref[sub]) for sub in range(subs)]
    for sub in range(subs):
        edge_ref[:, sub * width : (sub + 1) * width] = solved[sub]
    start = far_ref.shape[1]
    slot_sums(place_ref, len_ref, mult_ref, dof_ref, start, edge_ref, far_ref, *more)


def first_kernel(
    place_ref,
    len_ref,
    values_hbm,
    mult_hbm,
    dof_hbm,
    map_hbm,
    basis_hbm,
    inverse_hbm,
    scaled_ref,
    edge_ref,
    far_ref,
    own_ref,
    values_ref,
    mult_ref,
    dof_ref,
    map_ref,
    basis_ref,
    columns_ref,
    small_sems,
    sems,
):
    pairs = (
        (basis_hbm, basis_ref),
        (mult_hbm, mult_ref),
        (values_hbm, values_ref),
        (dof_hbm, dof_ref),
        (map_hbm, map_ref),
    )
    small = [
        pltpu.make_async_copy(source, target, small_sems.at[place])
        for place, (source, target) in enumerate(pairs)
    ]
    for copy in small:
        copy.start()
    copies = column_copies(inverse_hbm, columns_ref, sems, 0)

    @pl.when(started(place_ref))
    def _():
        for copy in small:
            copy.wait()
        for sub in range(values_ref.shape[0]):
            scaled = values_ref[sub].astype(jnp.float32) * weights_of(mult_ref[sub : sub + 1])
            scaled_ref[sub] = scaled.astype(jnp.bfloat16)
        edge_far(
            copies,
            place_ref,
            len_ref,
            mult_ref,
            dof_ref,
            scaled_ref,
            columns_ref,
            edge_ref,
            far_ref,
            basis_ref,
            map_ref,
            own_ref,
        )


def inner_kernel(
    place_ref,
    len_ref,
    scaled_ref,
    mult_ref,
    dof_ref,
    edge_ref,
    basis_ref,
    inverse_ref,
    *refs,
):
    *inputs, wide_ref, buffer_ref, sems = refs
    copies = column_copies(
        inverse_ref, buffer_ref, sems, inverse_ref.shape[2] - buffer_ref.shape[2]
    )
    if len(inputs) == 6:
        map_ref, after_ref, inner_ref, mate_ref, keep_ref, own_ref = inputs
        more = (basis_ref, map_ref, own_ref)
    else:
        after_ref, inner_ref, mate_ref, keep_ref = inputs
        more = (None, None, None)

    @pl.when(started(place_ref))
    def _():
        widen(basis_ref, wide_ref)
        keep, send = parts_of(place_ref, scaled_ref, wide_ref)
        half, entries = keep.shape
        keep_ref[...] = keep
        slot_sums(place_ref, len_ref, mult_ref, dof_ref, 0, edge_ref, mate_ref, *more)
        last = mate_ref.shape[0] - half // 2
        mate_ref[last:, :entries] = send[: half // 2]
        mate_ref[last:, entries : 2 * entries] = send[half // 2 :]

    for sub in range(scaled_ref.shape[0]):
        copies[sub].wait()
        inner_ref[sub] = mul(scaled_ref[sub], buffer_ref[sub])


def head_kernel(
    place_ref,
    len_ref,
    edge_ref,
    mate_ref,
    far_ref,
    from_mate_ref,
    from_far_ref,
    dof_ref,
    after_ref,
    *refs,
):
    subs, width = dof_ref.shape
    cases = edge_ref.shape[0]
    owned = mate_ref.shape[1]
    near = thirds(mate_ref[:cases] + from_mate_ref[:cases])
    far = thirds(far_ref[:cases] + from_far_ref[:cases])
    count = near.shape[0]
    if len(refs) == 1:
        (head_ref,) = refs
    else:
        basis_ref, own_mate_ref, own_far_ref, head_ref, shared_ref, map_ref, near_ref, wide_ref = refs
        coarse = basis_ref.shape[1]
        entries = own_mate_ref.shape[0]
        for ref, sums, own, arrived in (
            (near_ref, near, own_mate_ref, from_mate_ref),
            (wide_ref, far, own_far_ref, from_far_ref),
        ):
            ref[:count] = sums
            ref[count : count + entries] = own[...]
            row = arrived[cases + coarse : cases + coarse + 1]
            basis = arrived[cases : cases + coarse]
            for sub in range(subs):
                start = count + entries + sub * coarse
                ref[start : start + coarse] = jnp.where(row == float(sub), basis, 0.0).astype(
                    jnp.bfloat16
                )
        near, far = near_ref[...], wide_ref[...]
        row = cases + coarse + 8
        map_ref[0:1] = from_mate_ref[row : row + 1, :entries]
        map_ref[1:2] = from_far_ref[row : row + 1, :entries]
    for sub in range(subs):
        columns = slice(sub * width, (sub + 1) * width)
        hot = slots_of(place_ref, len_ref, dof_ref, sub, 2 * owned)
        by_mate = mul(near, hot[:owned])
        by_far = mul(far, hot[owned:])
        live = live_of(len_ref, sub, width)
        fetched = folded(by_mate[:count] + by_far[:count], cases)
        head_ref[:, columns] = jnp.where(live, fetched, edge_ref[:, columns])
        if len(refs) > 1:
            by_mate, by_far = by_mate[count:], by_far[count:]
            own = by_mate[:entries] + by_far[:entries]
            full = jnp.concatenate([own, by_mate[entries:], by_far[entries:]], axis=0)
            shared_ref[:, columns] = full.astype(jnp.bfloat16)
            rows = slice(sub * coarse, (sub + 1) * coarse)
            dead = jnp.where(live, 0.0, basis_ref[sub, :, :width].astype(jnp.float32))
            shared_ref[rows, columns] = (own[rows] + dead).astype(jnp.bfloat16)


def correct_kernel(
    place_ref,
    own_ref,
    near_ref,
    mine_ref,
    other_ref,
    basis_ref,
    head_ref,
    shared_ref,
    inner_ref,
    *refs,
):
    *inputs, wide_ref, values_ref, leave_sems = refs
    if len(inputs) == 1:
        (out_hbm,) = inputs
    else:
        (
            len_ref,
            mult_ref,
            dof_ref,
            inverse_hbm,
            out_hbm,
            scaled_ref,
            edge_ref,
            far_ref,
            columns_ref,
            sems,
        ) = inputs
        copies = column_copies(inverse_hbm, columns_ref, sems, 0)
    subs, cases, _ = values_ref.shape
    chips, half, _ = mine_ref.shape
    entries = near_ref.shape[1]
    width = head_ref.shape[1] // subs
    leave = [
        pltpu.make_async_copy(values_ref.at[sub], out_hbm.at[sub], leave_sems.at[sub])
        for sub in range(subs)
    ]

    @pl.when(started(place_ref))
    def _():
        widen(basis_ref, wide_ref)
        maps = jnp.concatenate([flat_map(own_ref), near_ref[0:1], near_ref[1:2]], axis=1)
        looked = jnp.zeros((4 * half, 3 * entries), jnp.float32)
        for pair in range(chips // 2):
            mine = jnp.concatenate([mine_ref[2 * pair], mine_ref[2 * pair + 1]], axis=1)
            other = jnp.concatenate([other_ref[2 * pair], other_ref[2 * pair + 1]], axis=1)
            both = halves(jnp.concatenate([mine, other], axis=0))
            looked = looked + mul(both, hot_pair(maps, pair))
        looked = folded(looked, cases)
        turned = jnp.concatenate([looked[half:], looked[:half]], axis=0)
        looked = jnp.where(lax.rem(place_ref[0], 2) == 0, looked, turned)
        own = thirds(looked[:, :entries])
        looked = thirds(looked)
        for sub in range(subs):
            columns = slice(sub * width, (sub + 1) * width)
            values_ref[sub, :, :width] = head_ref[:, columns] + folded(
                mul(looked, shared_ref[:, columns]), cases
            )
            values_ref[sub, :, width:] = inner_ref[sub] + folded(
                mul(own, wide_ref[sub, :, width:]), cases
            )
            leave[sub].start()
        if len(inputs) > 1:
            for sub in range(subs):
                scaled = values_ref[sub] * weights_of(mult_ref[sub : sub + 1])
                scaled_ref[sub] = scaled.astype(jnp.bfloat16)
            edge_far(
                copies,
                place_ref,
                len_ref,
                mult_ref,
                dof_ref,
                scaled_ref,
                columns_ref,
                edge_ref,
                far_ref,
                None,
                None,
                None,
            )

    for copy in leave:
        copy.wait()


def swap(value):
    return lax.ppermute(value, "c", [(0, 1), (1, 0)])


def far_swap(value):
    count = lax.axis_size(DOM)
    pairs = []
    for device in range(1, count, 2):
        after = (device + 1) % count
        pairs += [(device, after), (after, device)]
    return lax.ppermute(value, DOM, pairs)


def by_chip(value):
    return lax.all_to_all(value, CHIPS, 0, 0, tiled=True)


def local(
    residual_in,
    local_inverse,
    coarse_basis,
    coarse_inverse,
    multiplicity,
    iface_len,
    iface_dof,
    coarse_map,
):
    subs, cases, length = residual_in.shape
    coarse = coarse_basis.shape[1]
    width = iface_dof.shape[1]
    rows, order = coarse_inverse.shape
    chips = lax.axis_size(DOM) // 2
    half = cases // 2
    entries = subs * coarse
    spots = subs * width
    owned = spots // 2
    place = lax.axis_index(DOM).astype(jnp.int32).reshape(1)
    slot_flops = 2 * 3 * cases * spots * spots
    kept = cases + half // 2
    sent = kept + coarse + 16
    blocks = f32(chips, half, order // chips)
    inverse_bytes = 2 * local_inverse.size

    def buffers(count):
        return [
            pltpu.VMEM((subs, length, count), jnp.bfloat16),
            pltpu.SemaphoreType.DMA((subs,)),
        ]

    other_rows = swap(coarse_inverse)
    wide = pltpu.VMEM((subs, entries, length), jnp.bfloat16)
    opened = (bf16(subs, cases, length), f32(cases, spots))

    def dense(row, near, keep, arrived, *after):
        parts = call(
            functools.partial(dense_kernel, row),
            "dense",
            blocks,
            (coarse_map, near, keep, arrived, *after),
            [VMEM] * 4 + [ANY] * len(after),
        )
        return by_chip(parts)

    def inner_solve(scaled, edge, far, *more):
        outs = [f32(subs, cases, length - width), f32(sent if more else kept, owned)]
        outs.append(f32(half, entries))
        if more:
            outs.append(bf16(entries, owned))
        return call(
            inner_kernel,
            "inner",
            tuple(outs),
            (
                place,
                iface_len,
                scaled,
                multiplicity,
                iface_dof,
                edge,
                coarse_basis,
                local_inverse,
                *more,
                far,
            ),
            [SMEM] * 2 + [VMEM] * 5 + [HBM] + [VMEM] * len(more) + [ANY],
            flops=2 * scaled.size * (length - width) + slot_flops // 2,
            moved=inverse_bytes * 3 // 4,
            mib=60 if more else 50,
            scratch_shapes=[wide, *buffers(length - width)],
        )

    def coarse_solve(parts, after):
        rhs = call(
            sum_kernel, "sum", blocks, (parts, *after), [VMEM] + [ANY] * len(after)
        )
        rhs = by_chip(rhs)
        own = call(
            solve_kernel,
            "solve",
            blocks,
            (place, rhs, coarse_inverse, other_rows),
            [SMEM] + [VMEM] * 3,
        )
        return by_chip(own)

    def assemble(edge, mate, far, from_mate, from_far, after, *more):
        outs, scratch = [f32(cases, spots)], []
        if more:
            outs += [bf16(3 * entries, spots), f32(2, entries)]
            scratch = [pltpu.VMEM((3 * cases + 2 * entries, owned), jnp.bfloat16)] * 2
        return call(
            head_kernel,
            "head",
            tuple(outs),
            (place, iface_len, edge, mate, far, from_mate, from_far, iface_dof, after, *more),
            [SMEM] * 2 + [VMEM] * 6 + [ANY] + [VMEM] * len(more),
            flops=slot_flops,
            scratch_shapes=scratch,
        )

    def correct(mine, head, shared, inner, *more):
        outs, out_specs, specs, scratch = [f32(subs, cases, length)], [HBM], [], []
        if more:
            outs += [*opened, f32(kept, owned)]
            out_specs += [VMEM] * 3
            specs = [SMEM, VMEM, VMEM, HBM]
            scratch = buffers(width)
        return call(
            correct_kernel,
            "correct",
            tuple(outs),
            (
                place,
                coarse_map,
                near_maps,
                mine,
                swap(mine),
                coarse_basis,
                head,
                shared,
                inner,
                *more,
            ),
            [SMEM] + [VMEM] * 8 + specs,
            mib=50 if more else 16,
            out_specs=tuple(out_specs),
            scratch_shapes=[
                *scratch,
                wide,
                pltpu.VMEM((subs, cases, length), jnp.float32),
                pltpu.SemaphoreType.DMA((subs,)),
            ],
        )

    scaled, edge, far, own_far = call(
        first_kernel,
        "first",
        (*opened, f32(sent, owned), bf16(entries, owned)),
        (
            place,
            iface_len,
            residual_in,
            multiplicity,
            iface_dof,
            coarse_map,
            coarse_basis,
            local_inverse,
        ),
        [SMEM] * 2 + [HBM] * 6,
        mib=60,
        scratch_shapes=[
            pltpu.VMEM(residual_in.shape, jnp.bfloat16),
            pltpu.VMEM(multiplicity.shape, jnp.int32),
            pltpu.VMEM(iface_dof.shape, jnp.int32),
            pltpu.VMEM(coarse_map.shape, jnp.int32),
            pltpu.VMEM(coarse_basis.shape, jnp.bfloat16),
            buffers(width)[0],
            pltpu.SemaphoreType.DMA((5,)),
            buffers(width)[1],
        ],
    )
    from_far = far_swap(far)
    inner, mate, keep, own_mate = inner_solve(scaled, edge, far, coarse_map)
    from_mate = swap(mate)
    parts = dense(cases + coarse + 8, from_mate, keep, from_mate, from_far)
    head, shared, near_maps = assemble(
        edge, mate, far, from_mate, from_far, parts, coarse_basis, own_mate, own_far
    )
    mine = coarse_solve(parts, (head,))
    first_apply, scaled, edge, far = correct(
        mine, head, shared, inner, iface_len, multiplicity, iface_dof, local_inverse
    )

    from_far = far_swap(far)
    inner, mate, keep = inner_solve(scaled, edge, far)
    from_mate = swap(mate)
    parts = dense(0, near_maps, keep, from_mate, from_far)
    (head,) = assemble(edge, mate, far, from_mate, from_far, parts)
    mine = coarse_solve(parts, (head,))
    (second_apply,) = correct(mine, head, shared, inner)
    return first_apply, second_apply


def solution(mesh):
    grid = Mesh(mesh.devices.reshape(4, 4, 4, 2), DOM)
    placed = (
        P(DOM, None, None),
        P(DOM, None, None),
        P(DOM, None, None),
        P(DOM, None),
        P(DOM, None),
        P(DOM),
        P(DOM, None),
        P(DOM, None),
    )
    return jax.shard_map(
        local,
        mesh=grid,
        in_specs=placed,
        out_specs=(P(DOM, None, None), P(DOM, None, None)),
        check_vma=False,
    )
```

```python
import functools

import jax
import jax.numpy as jnp
from jax import lax
from jax.experimental import pallas as pl
from jax.experimental.pallas import tpu as pltpu
from jax.sharding import Mesh
from jax.sharding import PartitionSpec as P

CHIPS = ("y", "z", "x")
DOM = ("y", "z", "x", "c")
MIB = 2**20
VMEM = pl.BlockSpec(memory_space=pltpu.VMEM)
SMEM = pl.BlockSpec(memory_space=pltpu.SMEM)
ANY = pl.BlockSpec(memory_space=pl.ANY)
HBM = pl.BlockSpec(memory_space=pltpu.HBM)
BY_ROW = (((1,), (1,)), ((), ()))


def halves(value):
    high = value.astype(jnp.bfloat16)
    low = (value - high.astype(jnp.float32)).astype(jnp.bfloat16)
    return jnp.concatenate([high, low], axis=0)


def thirds(value):
    high = value.astype(jnp.bfloat16)
    rest = value - high.astype(jnp.float32)
    middle = rest.astype(jnp.bfloat16)
    low = (rest - middle.astype(jnp.float32)).astype(jnp.bfloat16)
    return jnp.concatenate([high, middle, low], axis=0)


def folded(out, rows):
    total = out[:rows]
    for start in range(rows, out.shape[0], rows):
        total = total + out[start : start + rows]
    return total


def mul(left, right):
    return jnp.dot(left, right, preferred_element_type=jnp.float32)


def mul_rows(left, right):
    return lax.dot_general(left, right, BY_ROW, preferred_element_type=jnp.float32)


def call(kernel, name, out_shape, args, specs, flops=1e6, moved=MIB, mib=16, **more):
    return pl.pallas_call(
        kernel,
        out_shape=out_shape,
        in_specs=specs,
        compiler_params=pltpu.CompilerParams(vmem_limit_bytes=mib * MIB),
        cost_estimate=pl.CostEstimate(
            flops=int(flops), bytes_accessed=int(moved), transcendentals=0
        ),
        name=name,
        **more,
    )(*args)


def f32(*shape):
    return jax.ShapeDtypeStruct(shape, jnp.float32)


def bf16(*shape):
    return jax.ShapeDtypeStruct(shape, jnp.bfloat16)


def weights_of(multiplicity):
    return 1.0 / multiplicity.astype(jnp.float32)


def parts_of(place_ref, scaled_ref, basis_ref):
    parts = mul_rows(scaled_ref[0], basis_ref[0])
    for sub in range(1, basis_ref.shape[0]):
        parts = parts + mul_rows(scaled_ref[sub], basis_ref[sub])
    half = parts.shape[0] // 2
    first = lax.rem(place_ref[0], 2) == 0
    keep = jnp.where(first, parts[:half], parts[half:])
    return keep, jnp.where(first, parts[half:], parts[:half])


def widen(basis_ref, wide_ref):
    subs, coarse, _ = basis_ref.shape
    for sub in range(subs):
        wide_ref[sub] = jnp.zeros_like(wide_ref[sub])
        wide_ref[sub, sub * coarse : (sub + 1) * coarse] = basis_ref[sub]


def flat_map(map_ref):
    subs, coarse = map_ref.shape
    entries = subs * coarse
    value = map_ref[...]
    digits = jnp.concatenate([lax.div(value, 128), lax.rem(value, 128)], axis=0)
    lane = lax.broadcasted_iota(jnp.int32, (coarse, entries), 1)
    row = lax.broadcasted_iota(jnp.int32, (coarse, entries), 0)
    spread = jnp.where(lax.rem(lane, coarse) == row, 1.0, 0.0).astype(jnp.bfloat16)
    digits = mul(digits.astype(jnp.float32).astype(jnp.bfloat16), spread)
    value = digits[:subs] * 128.0 + digits[subs:]
    lane = lax.broadcasted_iota(jnp.int32, (subs, entries), 1)
    row = lax.broadcasted_iota(jnp.int32, (subs, entries), 0)
    own = jnp.where(lax.div(lane, coarse) == row, value, 0.0)
    return jnp.sum(own, axis=0, keepdims=True)


def hot_pair(maps, pair):
    rows = lax.broadcasted_iota(jnp.int32, (256, maps.shape[1]), 0) + 256 * pair
    return jnp.where(rows.astype(jnp.float32) == maps, 1.0, 0.0).astype(jnp.bfloat16)


def columns_of(rows):
    if rows.shape[0] == 1:
        rows = jnp.broadcast_to(rows, (8, rows.shape[1]))
    return rows.astype(jnp.float32).T


def dense_kernel(row, own_ref, near_ref, keep_ref, arrived_ref, *refs):
    out_ref = refs[-1]
    cases, width = keep_ref.shape
    got = arrived_ref[arrived_ref.shape[0] - cases // 2 :, : 2 * width]
    got = jnp.concatenate([got[:, :width], got[:, width:]], axis=0)
    value = halves(jnp.concatenate([keep_ref[...], got], axis=1))
    mate = near_ref[row : row + 1, :width]
    maps = jnp.concatenate([flat_map(own_ref), mate], axis=1)
    maps = columns_of(maps)[:, :1]
    wide = 2 * out_ref.shape[2]
    for pair in range(out_ref.shape[0] // 2):
        numbers = lax.broadcasted_iota(jnp.int32, (maps.shape[0], wide), 1) + wide * pair
        hot = jnp.where(numbers.astype(jnp.float32) == maps, 1.0, 0.0).astype(jnp.bfloat16)
        part = folded(mul(value, hot), cases)
        out_ref[2 * pair] = part[:, : wide // 2]
        out_ref[2 * pair + 1] = part[:, wide // 2 :]


def sum_kernel(parts_ref, *refs):
    out_ref = refs[-1]
    total = parts_ref[0]
    for chip in range(1, parts_ref.shape[0]):
        total = total + parts_ref[chip]
    for chip in range(out_ref.shape[0]):
        out_ref[chip] = total


def solve_kernel(place_ref, rhs_ref, mine_ref, other_ref, out_ref):
    cases, width = rhs_ref.shape[1:]
    total = jnp.zeros((2 * cases, 4 * mine_ref.shape[0]), jnp.float32)
    for pair in range(rhs_ref.shape[0] // 2):
        value = jnp.concatenate([rhs_ref[2 * pair], rhs_ref[2 * pair + 1]], axis=1)
        columns = slice(2 * pair * width, 2 * (pair + 1) * width)
        rows = jnp.concatenate([mine_ref[:, columns], other_ref[:, columns]], axis=0)
        total = total + mul_rows(halves(value), halves(rows))
    total = folded(total, cases)
    own = total[:, :width] + total[:, width:]
    half = width // 2
    turned = jnp.concatenate([own[:, half:], own[:, :half]], axis=1)
    own = jnp.where(lax.rem(place_ref[0], 2) == 0, own, turned)
    for chip in range(out_ref.shape[0]):
        out_ref[chip] = own


def live_of(len_ref, sub, width):
    return lax.broadcasted_iota(jnp.int32, (1, width), 1) < len_ref[sub]


def slot_row(place_ref, len_ref, dof_ref, sub, spots):
    owned = spots // 2
    dof = dof_ref[sub : sub + 1]
    owner = lax.div(dof, owned)
    away = (owner != place_ref[0]).astype(jnp.int32)
    far = jnp.where(lax.rem(place_ref[0], 2) == 0, away, 1 - away)
    live = live_of(len_ref, sub, dof.shape[1])
    return jnp.where(live, far * owned + (dof - owner * owned), -1)


def slots_of(place_ref, len_ref, dof_ref, sub, spots):
    slot = slot_row(place_ref, len_ref, dof_ref, sub, spots)
    rows = lax.broadcasted_iota(jnp.int32, (spots, slot.shape[1]), 0)
    return jnp.where(rows == slot, 1.0, 0.0).astype(jnp.bfloat16)


def started(place_ref):
    return place_ref[0] >= 0


def column_copies(inverse_ref, buffer_ref, sems, start):
    copies = []
    for sub in range(inverse_ref.shape[0]):
        columns = pl.ds(start, buffer_ref.shape[2])
        copies.append(
            pltpu.make_async_copy(
                inverse_ref.at[sub, :, columns], buffer_ref.at[sub], sems.at[sub]
            )
        )
    for copy in copies:
        copy.start()
    return copies


def interface(len_ref, mult_ref, sub, width):
    live = live_of(len_ref, sub, width)
    return live, jnp.where(live, weights_of(mult_ref[sub : sub + 1, :width]), 0.0)


def slot_sums(
    place_ref, len_ref, mult_ref, dof_ref, start, edge_ref, sums_ref, basis_ref, map_ref, own_ref
):
    subs, width = dof_ref.shape
    owned = sums_ref.shape[1]
    slots = [slot_row(place_ref, len_ref, dof_ref, sub, 2 * owned) for sub in range(subs)]
    slots = columns_of(jnp.concatenate(slots, axis=0))
    numbers = lax.broadcasted_iota(jnp.int32, (width, owned), 1) + start
    numbers = numbers.astype(jnp.float32)
    total = None
    for sub in range(subs):
        live, mask = interface(len_ref, mult_ref, sub, width)
        hot = jnp.where(numbers == slots[:, sub : sub + 1], 1.0, 0.0).astype(jnp.bfloat16)
        solved = edge_ref[:, sub * width : (sub + 1) * width]
        cases = solved.shape[0]
        pieces = [thirds(solved * mask)]
        if basis_ref is not None:
            coarse = basis_ref.shape[1]
            weighted = basis_ref[sub, :, :width].astype(jnp.float32) * mask
            pieces.append(weighted.astype(jnp.bfloat16))
            number = jnp.where(live, float(sub), 0.0).astype(jnp.bfloat16)
            pieces.append(jnp.broadcast_to(number, (16, width)))
        out = mul(jnp.concatenate(pieces, axis=0), hot)
        moved = folded(out[: 3 * cases], cases)
        if basis_ref is not None:
            rest = out[3 * cases : 3 * cases + coarse + 8]
            own_ref[sub * coarse : (sub + 1) * coarse, :] = rest[:coarse].astype(jnp.bfloat16)
            moved = jnp.concatenate([moved, rest], axis=0)
        total = moved if total is None else total + moved
    count = total.shape[0]
    sums_ref[:count] = total
    sums_ref[count:] = jnp.zeros_like(sums_ref[count:])
    if basis_ref is not None:
        flat = flat_map(map_ref)
        sums_ref[count : count + 1, : flat.shape[1]] = flat


def edge_far(
    copies, place_ref, len_ref, mult_ref, dof_ref, scaled_ref, columns_ref, edge_ref, far_ref, *more
):
    subs, width = dof_ref.shape
    for copy in copies:
        copy.wait()
    solved = [mul(scaled_ref[sub], columns_ref[sub]) for sub in range(subs)]
    for sub in range(subs):
        edge_ref[:, sub * width : (sub + 1) * width] = solved[sub]
    start = far_ref.shape[1]
    slot_sums(place_ref, len_ref, mult_ref, dof_ref, start, edge_ref, far_ref, *more)


def first_kernel(
    place_ref,
    len_ref,
    values_hbm,
    mult_hbm,
    dof_hbm,
    map_hbm,
    basis_hbm,
    inverse_hbm,
    scaled_ref,
    edge_ref,
    far_ref,
    own_ref,
    values_ref,
    mult_ref,
    dof_ref,
    map_ref,
    basis_ref,
    columns_ref,
    small_sems,
    sems,
):
    pairs = (
        (basis_hbm, basis_ref),
        (mult_hbm, mult_ref),
        (values_hbm, values_ref),
        (dof_hbm, dof_ref),
        (map_hbm, map_ref),
    )
    small = [
        pltpu.make_async_copy(source, target, small_sems.at[place])
        for place, (source, target) in enumerate(pairs)
    ]
    for copy in small:
        copy.start()
    copies = column_copies(inverse_hbm, columns_ref, sems, 0)

    @pl.when(started(place_ref))
    def _():
        for copy in small:
            copy.wait()
        for sub in range(values_ref.shape[0]):
            scaled = values_ref[sub].astype(jnp.float32) * weights_of(mult_ref[sub : sub + 1])
            scaled_ref[sub] = scaled.astype(jnp.bfloat16)
        edge_far(
            copies,
            place_ref,
            len_ref,
            mult_ref,
            dof_ref,
            scaled_ref,
            columns_ref,
            edge_ref,
            far_ref,
            basis_ref,
            map_ref,
            own_ref,
        )


def inner_kernel(
    place_ref,
    len_ref,
    scaled_ref,
    mult_ref,
    dof_ref,
    edge_ref,
    basis_ref,
    inverse_ref,
    *refs,
):
    *inputs, wide_ref, buffer_ref, sems = refs
    small = []
    if len(inputs) == 13:
        map_ref, after_ref, inner_ref, mate_ref, keep_ref, own_ref, *held, small_sems = inputs
        given = (scaled_ref, mult_ref, dof_ref, edge_ref, basis_ref, map_ref)
        small = [
            pltpu.make_async_copy(source, target, small_sems.at[place])
            for place, (source, target) in enumerate(zip(given, held))
        ]
        for copy in small:
            copy.start()
        scaled_ref, mult_ref, dof_ref, edge_ref, basis_ref, map_ref = held
        more = (basis_ref, map_ref, own_ref)
    else:
        after_ref, inner_ref, mate_ref, keep_ref = inputs
        more = (None, None, None)
    copies = column_copies(
        inverse_ref, buffer_ref, sems, inverse_ref.shape[2] - buffer_ref.shape[2]
    )

    @pl.when(started(place_ref))
    def _():
        for copy in small:
            copy.wait()
        widen(basis_ref, wide_ref)
        keep, send = parts_of(place_ref, scaled_ref, wide_ref)
        half, entries = keep.shape
        keep_ref[...] = keep
        slot_sums(place_ref, len_ref, mult_ref, dof_ref, 0, edge_ref, mate_ref, *more)
        last = mate_ref.shape[0] - half // 2
        mate_ref[last:, :entries] = send[: half // 2]
        mate_ref[last:, entries : 2 * entries] = send[half // 2 :]

    for sub in range(scaled_ref.shape[0]):
        copies[sub].wait()
        inner_ref[sub] = mul(scaled_ref[sub], buffer_ref[sub])


def head_kernel(
    place_ref,
    len_ref,
    edge_ref,
    mate_ref,
    far_ref,
    from_mate_ref,
    from_far_ref,
    dof_ref,
    after_ref,
    *refs,
):
    subs, width = dof_ref.shape
    cases = edge_ref.shape[0]
    owned = mate_ref.shape[1]
    near = thirds(mate_ref[:cases] + from_mate_ref[:cases])
    far = thirds(far_ref[:cases] + from_far_ref[:cases])
    count = near.shape[0]
    if len(refs) == 1:
        (head_ref,) = refs
    else:
        basis_ref, own_mate_ref, own_far_ref, head_ref, shared_ref, map_ref, near_ref, wide_ref = refs
        coarse = basis_ref.shape[1]
        entries = own_mate_ref.shape[0]
        for ref, sums, own, arrived in (
            (near_ref, near, own_mate_ref, from_mate_ref),
            (wide_ref, far, own_far_ref, from_far_ref),
        ):
            ref[:count] = sums
            ref[count : count + entries] = own[...]
            row = arrived[cases + coarse : cases + coarse + 1]
            basis = arrived[cases : cases + coarse]
            for sub in range(subs):
                start = count + entries + sub * coarse
                ref[start : start + coarse] = jnp.where(row == float(sub), basis, 0.0).astype(
                    jnp.bfloat16
                )
        near, far = near_ref[...], wide_ref[...]
        row = cases + coarse + 8
        map_ref[0:1] = from_mate_ref[row : row + 1, :entries]
        map_ref[1:2] = from_far_ref[row : row + 1, :entries]
    for sub in range(subs):
        columns = slice(sub * width, (sub + 1) * width)
        hot = slots_of(place_ref, len_ref, dof_ref, sub, 2 * owned)
        by_mate = mul(near, hot[:owned])
        by_far = mul(far, hot[owned:])
        live = live_of(len_ref, sub, width)
        fetched = folded(by_mate[:count] + by_far[:count], cases)
        head_ref[:, columns] = jnp.where(live, fetched, edge_ref[:, columns])
        if len(refs) > 1:
            by_mate, by_far = by_mate[count:], by_far[count:]
            own = by_mate[:entries] + by_far[:entries]
            full = jnp.concatenate([own, by_mate[entries:], by_far[entries:]], axis=0)
            shared_ref[:, columns] = full.astype(jnp.bfloat16)
            rows = slice(sub * coarse, (sub + 1) * coarse)
            dead = jnp.where(live, 0.0, basis_ref[sub, :, :width].astype(jnp.float32))
            shared_ref[rows, columns] = (own[rows] + dead).astype(jnp.bfloat16)


def correct_kernel(
    place_ref,
    own_ref,
    near_ref,
    mine_ref,
    other_ref,
    basis_ref,
    head_ref,
    shared_ref,
    inner_ref,
    *refs,
):
    *inputs, wide_ref, values_ref, leave_sems = refs
    if len(inputs) == 1:
        (out_hbm,) = inputs
    else:
        (
            len_ref,
            mult_ref,
            dof_ref,
            inverse_hbm,
            out_hbm,
            scaled_ref,
            edge_ref,
            far_ref,
            columns_ref,
            sems,
        ) = inputs
        copies = column_copies(inverse_hbm, columns_ref, sems, 0)
    subs, cases, _ = values_ref.shape
    chips, half, _ = mine_ref.shape
    entries = near_ref.shape[1]
    width = head_ref.shape[1] // subs
    leave = [
        pltpu.make_async_copy(values_ref.at[sub], out_hbm.at[sub], leave_sems.at[sub])
        for sub in range(subs)
    ]

    @pl.when(started(place_ref))
    def _():
        widen(basis_ref, wide_ref)
        maps = jnp.concatenate([flat_map(own_ref), near_ref[0:1], near_ref[1:2]], axis=1)
        looked = jnp.zeros((4 * half, 3 * entries), jnp.float32)
        for pair in range(chips // 2):
            mine = jnp.concatenate([mine_ref[2 * pair], mine_ref[2 * pair + 1]], axis=1)
            other = jnp.concatenate([other_ref[2 * pair], other_ref[2 * pair + 1]], axis=1)
            both = halves(jnp.concatenate([mine, other], axis=0))
            looked = looked + mul(both, hot_pair(maps, pair))
        looked = folded(looked, cases)
        turned = jnp.concatenate([looked[half:], looked[:half]], axis=0)
        looked = jnp.where(lax.rem(place_ref[0], 2) == 0, looked, turned)
        own = thirds(looked[:, :entries])
        looked = thirds(looked)
        for sub in range(subs):
            columns = slice(sub * width, (sub + 1) * width)
            values_ref[sub, :, :width] = head_ref[:, columns] + folded(
                mul(looked, shared_ref[:, columns]), cases
            )
            values_ref[sub, :, width:] = inner_ref[sub] + folded(
                mul(own, wide_ref[sub, :, width:]), cases
            )
            leave[sub].start()
        if len(inputs) > 1:
            for sub in range(subs):
                scaled = values_ref[sub] * weights_of(mult_ref[sub : sub + 1])
                scaled_ref[sub] = scaled.astype(jnp.bfloat16)
            edge_far(
                copies,
                place_ref,
                len_ref,
                mult_ref,
                dof_ref,
                scaled_ref,
                columns_ref,
                edge_ref,
                far_ref,
                None,
                None,
                None,
            )

    for copy in leave:
        copy.wait()


def swap(value):
    return lax.ppermute(value, "c", [(0, 1), (1, 0)])


def far_swap(value):
    count = lax.axis_size(DOM)
    pairs = []
    for device in range(1, count, 2):
        after = (device + 1) % count
        pairs += [(device, after), (after, device)]
    return lax.ppermute(value, DOM, pairs)


def by_chip(value):
    return lax.all_to_all(value, CHIPS, 0, 0, tiled=True)


def local(
    residual_in,
    local_inverse,
    coarse_basis,
    coarse_inverse,
    multiplicity,
    iface_len,
    iface_dof,
    coarse_map,
):
    subs, cases, length = residual_in.shape
    coarse = coarse_basis.shape[1]
    width = iface_dof.shape[1]
    rows, order = coarse_inverse.shape
    chips = lax.axis_size(DOM) // 2
    half = cases // 2
    entries = subs * coarse
    spots = subs * width
    owned = spots // 2
    place = lax.axis_index(DOM).astype(jnp.int32).reshape(1)
    slot_flops = 2 * 3 * cases * spots * spots
    kept = cases + half // 2
    sent = kept + coarse + 16
    blocks = f32(chips, half, order // chips)
    inverse_bytes = 2 * local_inverse.size

    def buffers(count):
        return [
            pltpu.VMEM((subs, length, count), jnp.bfloat16),
            pltpu.SemaphoreType.DMA((subs,)),
        ]

    other_rows = swap(coarse_inverse)
    wide = pltpu.VMEM((subs, entries, length), jnp.bfloat16)
    opened = (bf16(subs, cases, length), f32(cases, spots))

    def dense(row, near, keep, arrived, *after):
        parts = call(
            functools.partial(dense_kernel, row),
            "dense",
            blocks,
            (coarse_map, near, keep, arrived, *after),
            [VMEM] * 4 + [ANY] * len(after),
        )
        return by_chip(parts)

    def inner_solve(scaled, edge, far, *more):
        outs = [f32(subs, cases, length - width), f32(sent if more else kept, owned)]
        outs.append(f32(half, entries))
        held = []
        if more:
            arrays = (scaled, multiplicity, iface_dof, edge, coarse_basis, coarse_map)
            held = [pltpu.VMEM(array.shape, array.dtype) for array in arrays]
            held.append(pltpu.SemaphoreType.DMA((len(arrays),)))
        if more:
            outs.append(bf16(entries, owned))
        return call(
            inner_kernel,
            "inner",
            tuple(outs),
            (
                place,
                iface_len,
                scaled,
                multiplicity,
                iface_dof,
                edge,
                coarse_basis,
                local_inverse,
                *more,
                far,
            ),
            [SMEM] * 2 + [HBM if more else VMEM] * 5 + [HBM] * (1 + len(more)) + [ANY],
            flops=2 * scaled.size * (length - width) + slot_flops // 2,
            moved=inverse_bytes * 3 // 4,
            mib=60 if more else 50,
            scratch_shapes=[*held, wide, *buffers(length - width)],
        )

    def coarse_solve(parts, after):
        rhs = call(
            sum_kernel, "sum", blocks, (parts, *after), [VMEM] + [ANY] * len(after)
        )
        rhs = by_chip(rhs)
        own = call(
            solve_kernel,
            "solve",
            blocks,
            (place, rhs, coarse_inverse, other_rows),
            [SMEM] + [VMEM] * 3,
        )
        return by_chip(own)

    def assemble(edge, mate, far, from_mate, from_far, after, *more):
        outs, scratch = [f32(cases, spots)], []
        if more:
            outs += [bf16(3 * entries, spots), f32(2, entries)]
            scratch = [pltpu.VMEM((3 * cases + 2 * entries, owned), jnp.bfloat16)] * 2
        return call(
            head_kernel,
            "head",
            tuple(outs),
            (place, iface_len, edge, mate, far, from_mate, from_far, iface_dof, after, *more),
            [SMEM] * 2 + [VMEM] * 6 + [ANY] + [VMEM] * len(more),
            flops=slot_flops,
            scratch_shapes=scratch,
        )

    def correct(mine, head, shared, inner, *more):
        outs, out_specs, specs, scratch = [f32(subs, cases, length)], [HBM], [], []
        if more:
            outs += [*opened, f32(kept, owned)]
            out_specs += [VMEM] * 3
            specs = [SMEM, VMEM, VMEM, HBM]
            scratch = buffers(width)
        return call(
            correct_kernel,
            "correct",
            tuple(outs),
            (
                place,
                coarse_map,
                near_maps,
                mine,
                swap(mine),
                coarse_basis,
                head,
                shared,
                inner,
                *more,
            ),
            [SMEM] + [VMEM] * 8 + specs,
            mib=50 if more else 16,
            out_specs=tuple(out_specs),
            scratch_shapes=[
                *scratch,
                wide,
                pltpu.VMEM((subs, cases, length), jnp.float32),
                pltpu.SemaphoreType.DMA((subs,)),
            ],
        )

    scaled, edge, far, own_far = call(
        first_kernel,
        "first",
        (*opened, f32(sent, owned), bf16(entries, owned)),
        (
            place,
            iface_len,
            residual_in,
            multiplicity,
            iface_dof,
            coarse_map,
            coarse_basis,
            local_inverse,
        ),
        [SMEM] * 2 + [HBM] * 6,
        mib=60,
        scratch_shapes=[
            pltpu.VMEM(residual_in.shape, jnp.bfloat16),
            pltpu.VMEM(multiplicity.shape, jnp.int32),
            pltpu.VMEM(iface_dof.shape, jnp.int32),
            pltpu.VMEM(coarse_map.shape, jnp.int32),
            pltpu.VMEM(coarse_basis.shape, jnp.bfloat16),
            buffers(width)[0],
            pltpu.SemaphoreType.DMA((5,)),
            buffers(width)[1],
        ],
    )
    from_far = far_swap(far)
    inner, mate, keep, own_mate = inner_solve(scaled, edge, far, coarse_map)
    from_mate = swap(mate)
    parts = dense(cases + coarse + 8, from_mate, keep, from_mate, from_far)
    head, shared, near_maps = assemble(
        edge, mate, far, from_mate, from_far, parts, coarse_basis, own_mate, own_far
    )
    mine = coarse_solve(parts, (head,))
    first_apply, scaled, edge, far = correct(
        mine, head, shared, inner, iface_len, multiplicity, iface_dof, local_inverse
    )

    from_far = far_swap(far)
    inner, mate, keep = inner_solve(scaled, edge, far)
    from_mate = swap(mate)
    parts = dense(0, near_maps, keep, from_mate, from_far)
    (head,) = assemble(edge, mate, far, from_mate, from_far, parts)
    mine = coarse_solve(parts, (head,))
    (second_apply,) = correct(mine, head, shared, inner)
    return first_apply, second_apply


def solution(mesh):
    grid = Mesh(mesh.devices.reshape(4, 4, 4, 2), DOM)
    placed = (
        P(DOM, None, None),
        P(DOM, None, None),
        P(DOM, None, None),
        P(DOM, None),
        P(DOM, None),
        P(DOM),
        P(DOM, None),
        P(DOM, None),
    )
    return jax.shard_map(
        local,
        mesh=grid,
        in_specs=placed,
        out_specs=(P(DOM, None, None), P(DOM, None, None)),
        check_vma=False,
    )
```
